128 devices in a mesh: grp: 8 (over z_hi, x), ctx: 16 (over z_lo, y, core).
Axes of the slice: x: 4, y: 4, z: 4 (z_hi: 2, z_lo: 2; z = z_hi * 2 + z_lo), core: 2. Of those that a mesh axis runs over, the one named last changes fastest.
Arguments:
- acts: bfloat16 [8, 16, 128, 2048], P('grp', 'ctx'), may hold values from -6 to 6
- doc_lengths: int32 [8, 2], P('grp'), may hold values from 256 to 1792, as said below
- w_query: bfloat16 [2048, 2048], P(None, 'ctx'), may hold values from -0.125 to 0.125
- w_key: bfloat16 [2048, 2048], P(None, 'ctx'), may hold values from -0.125 to 0.125
- w_value: bfloat16 [2048, 2048], P(None, 'ctx'), may hold values from -0.125 to 0.125
- w_out: bfloat16 [2048, 2048], P('ctx'), may hold values from -6 to 6
- w_gate: bfloat16 [2048, 5504], P(None, 'ctx'), may hold values from -0.125 to 0.125
- w_up: bfloat16 [2048, 5504], P(None, 'ctx'), may hold values from -0.125 to 0.125
- w_down: bfloat16 [5504, 2048], P('ctx'), may hold values from -0.078125 to 0.078125
- gain_attn: bfloat16 [2048], P('ctx'), may hold values from 0.5 to 1.5
- gain_mlp: bfloat16 [2048], P('ctx'), may hold values from 0.5 to 1.5
- cotangent: bfloat16 [8, 16, 128, 2048], P('grp', 'ctx'), may hold values from -6 to 6
Outputs:
- mixed: bfloat16 [8, 16, 128, 2048], P('grp', 'ctx')
- acts_grad: float32 [8, 16, 128, 2048], P('grp', 'ctx')
- grad_query: float32 [2048, 2048], P(None, 'ctx')
- grad_key: float32 [2048, 2048], P(None, 'ctx')
- grad_value: float32 [2048, 2048], P(None, 'ctx')
- grad_out: float32 [2048, 2048], P('ctx')
- grad_gate: float32 [2048, 5504], P(None, 'ctx')
- grad_up: float32 [2048, 5504], P(None, 'ctx')
- grad_down: float32 [5504, 2048], P('ctx')
- grad_gain_attn: float32 [2048], P('ctx')
- grad_gain_mlp: float32 [2048], P('ctx')
The draws below stay inside these ranges and needn't reach their ends.
Inputs may be any that keep to these rules, and one draw needn't show every extreme that they name: `doc_lengths`: in each group the two lengths sum to 2048 and one of them is at least 1536; either may come first.
All inputs are finite; a program needn't handle non-finite values.
Results may differ from the reference program's by a relative error of at most 0.028.
Values may be sent and summed in bfloat16 or wider, within the bound.
A program may use at most 384 MiB of HBM per device.

```python
import math
import jax
import jax.numpy as jnp
from jax import lax

D = 2048
HEADS = 16
FF = 5504
TOK_DEV = 128
ROW = 2048
N_GRP = 8
N_CTX = 16


def draw_doc_lengths(key, part):
    key = jax.random.fold_in(key, 11)
    key_order, key_side = jax.random.split(key)
    order_perm = jax.random.permutation(key_order, N_GRP).astype(jnp.int32)
    eighth = ROW // 8
    short_len = eighth + order_perm * eighth // N_GRP
    long_first = jax.random.randint(key_side, (N_GRP,), 0, 2)
    leading = jnp.where(long_first == 1, ROW - short_len, short_len)
    return jnp.stack([leading, ROW - leading], 1).astype(jnp.int32)


def level_of(own_key, shape, cuts, low, top_value):
    def one(dim, shards_of):
        heights = jax.random.uniform(jax.random.fold_in(jax.random.fold_in(own_key, 6), dim), (shards_of,), jnp.float32, low / len(cuts), top_value / len(cuts))
        return jnp.repeat(jnp.exp(heights), shape[dim] // shards_of).reshape((-1,) + (1,) * (len(shape) - dim - 1))

    level = one(*cuts[0])
    for cut in cuts[1:]:
        level = level * one(*cut)
    return level


def centred(key, extent, deviation, most, shards=(), kind=jnp.bfloat16):
    factor_of = level_of(key, extent, shards, -0.22, 0.18) if shards else 1.0
    array = jax.random.normal(key, extent, jnp.float32) * deviation * factor_of
    return jnp.minimum(jnp.maximum(array, -most), most).astype(kind)


def setup_inputs(seed: int = 0) -> dict:
    arg_keys = jax.random.split(jax.random.key(seed), 13)
    acts = centred(arg_keys[0], (N_GRP, N_CTX, TOK_DEV, D), 1.0, 6.0, ((0, 8), (1, 16)))
    doc_lengths = draw_doc_lengths(jax.random.fold_in(arg_keys[12], 71), 0)
    w_query = centred(arg_keys[2], (D, D), D ** -0.5, 0.125, ((1, 16),))
    w_key = centred(arg_keys[3], (D, D), D ** -0.5, 0.125, ((1, 16),))
    w_value = centred(arg_keys[4], (D, D), D ** -0.5, 0.125, ((1, 16),))
    w_out = centred(arg_keys[5], (D, D), 1.0, 6.0, ((0, 16),))
    w_gate = centred(arg_keys[6], (D, FF), D ** -0.5, 0.125, ((1, 16),))
    w_up = centred(arg_keys[7], (D, FF), D ** -0.5, 0.125, ((1, 16),))
    w_down = centred(arg_keys[8], (FF, D), FF ** -0.5, 0.078125, ((0, 16),))
    gain_attn = jnp.clip(1.0 + 0.1 * jax.random.normal(arg_keys[9], (D,), jnp.float32), 0.5, 1.5).astype(jnp.bfloat16)
    gain_mlp = jnp.clip(1.0 + 0.1 * jax.random.normal(arg_keys[10], (D,), jnp.float32), 0.5, 1.5).astype(jnp.bfloat16)
    cotangent = centred(arg_keys[11], (N_GRP, N_CTX, TOK_DEV, D), 1.0, 6.0, ((0, 8), (1, 16)))
    return dict(acts=acts, doc_lengths=doc_lengths, w_query=w_query, w_key=w_key, w_value=w_value, w_out=w_out, w_gate=w_gate, w_up=w_up, w_down=w_down, gain_attn=gain_attn, gain_mlp=gain_mlp, cotangent=cotangent)


@jax.custom_vjp
def low(v):
    return lax.optimization_barrier(v.astype(jnp.bfloat16)).astype(jnp.float32)

@jax.custom_vjp
def low_back(v):
    return v

def low_keep(v):
    return (low(v), None)

def low_pass(kept, grad):
    return (grad,)

def back_keep(v):
    return (v, None)

def back_low(kept, grad):
    return (low(grad),)
low.defvjp(low_keep, low_pass)
low_back.defvjp(back_keep, back_low)
EPSILON = 1e-05

def matmul(left, right):
    return jnp.dot(left, right, precision=lax.Precision.HIGHEST, preferred_element_type=jnp.float32)

def rms_norm(tensor, gain):
    return tensor * lax.rsqrt(lax.optimization_barrier(jnp.mean(tensor * tensor, -1, keepdims=True)) + EPSILON) * gain

def rotary(offsets, head_size):
    frequency = 10000.0 ** (-(jnp.arange(head_size // 2).astype(jnp.float32) * 2.0 / head_size))
    angles = offsets.astype(jnp.float32)[:, None] * frequency[None, :]
    return (jnp.cos(angles)[:, None, :], jnp.sin(angles)[:, None, :])

def rotate(tensor, cosine, sine_table):
    middle = tensor.shape[-1] // 2
    first_half = tensor[..., :middle]
    second = tensor[..., middle:]
    return jnp.concatenate([first_half * cosine - second * sine_table, second * cosine + first_half * sine_table], -1)

def to_rows(packed):
    groups, ctx_count, tok_dev, model_width = packed.shape
    middle = tok_dev // 2
    split_view = packed.reshape(groups, ctx_count, 2, middle, model_width)
    front_half = split_view[:, :, 0]
    back_half = split_view[:, ::-1, 1]
    return jnp.concatenate([front_half, back_half], 1).reshape(groups, 2 * ctx_count * middle, model_width)

def to_packed(sequence, ctx_count):
    groups, length, model_width = sequence.shape
    middle = length // (2 * ctx_count)
    split_view = sequence.reshape(groups, 2 * ctx_count, middle, model_width)
    front_half = split_view[:, :ctx_count]
    back_half = split_view[:, ctx_count:][:, ::-1]
    return jnp.stack([front_half, back_half], 2).reshape(groups, ctx_count, 2 * middle, model_width)

def layer(tokens, lengths, weights):
    w_query, w_key, w_value, w_out, w_gate, w_up, w_down, gain_attn, gain_mlp = weights
    length, model_width = tokens.shape
    head_size = model_width // HEADS
    scale_factor = 1.0 / math.sqrt(head_size)
    position = jnp.arange(length, dtype=jnp.int32)
    document = (position >= lengths[0]).astype(jnp.int32)
    offsets = position - document * lengths[0]
    own_length = jnp.where(document == 0, lengths[0], lengths[1])
    bias_term = -jnp.log(own_length.astype(jnp.float32))
    cosine, sine_table = rotary(offsets, head_size)
    normed = low(rms_norm(tokens, gain_attn))
    proj_query = low_back(matmul(normed, w_query))
    proj_key = low_back(matmul(normed, w_key))
    proj_value = low(low_back(matmul(normed, w_value)))
    q_rot = low(rotate(proj_query.reshape(length, HEADS, head_size), cosine, sine_table))
    k_rot = low(rotate(proj_key.reshape(length, HEADS, head_size), cosine, sine_table))
    v_heads = proj_value.reshape(length, HEADS, head_size)
    block_rows = math.gcd(512, length)
    block_count = length // block_rows

    def attend(pieces):
        q_block, pos_block, doc_block, bias_block = pieces
        score = jnp.einsum('qhd,khd->hqk', q_block, k_rot, precision=lax.Precision.HIGHEST) * scale_factor
        score = low_back(score + bias_block[None, :, None])
        visible = ((document[None, :] == doc_block[:, None]) & (position[None, :] <= pos_block[:, None])).astype(jnp.float32)
        attn_probs = low(jax.nn.sigmoid(score) * visible[None])
        return jnp.einsum('hqk,khd->qhd', attn_probs, v_heads, precision=lax.Precision.HIGHEST)
    attended = lax.map(jax.checkpoint(attend), (q_rot.reshape(block_count, block_rows, HEADS, head_size), position.reshape(block_count, block_rows), document.reshape(block_count, block_rows), bias_term.reshape(block_count, block_rows)))
    attended = low(low_back(attended.reshape(length, model_width)))
    residual = tokens + low_back(matmul(attended, w_out))
    normed_two = low(rms_norm(residual, gain_mlp))
    gate_proj = low_back(matmul(normed_two, w_gate))
    up_proj = low_back(matmul(normed_two, w_up))
    hidden = low(jax.nn.silu(gate_proj) * up_proj)
    return residual + matmul(hidden, w_down)

def reference(acts, doc_lengths, w_query, w_key, w_value, w_out, w_gate, w_up, w_down, gain_attn, gain_mlp, cotangent):
    weights = (w_query.astype(jnp.float32), w_key.astype(jnp.float32), w_value.astype(jnp.float32), w_out.astype(jnp.float32), w_gate.astype(jnp.float32), w_up.astype(jnp.float32), w_down.astype(jnp.float32), gain_attn.astype(jnp.float32), gain_mlp.astype(jnp.float32))
    sequence = to_rows(acts.astype(jnp.float32))
    cot_rows = to_rows(cotangent.astype(jnp.float32))

    def forward(rows_in, params):

        def one_group(item):
            return layer(item[0], item[1], params)
        return lax.map(jax.checkpoint(one_group), (rows_in, doc_lengths))
    result, pull = jax.vjp(forward, sequence, weights)
    d_rows, d_params = pull(cot_rows)
    mixed = to_packed(result, N_CTX).astype(jnp.bfloat16)
    acts_grad = to_packed(d_rows, N_CTX)
    return (mixed, acts_grad, d_params[0], d_params[1], d_params[2], d_params[3], d_params[4], d_params[5], d_params[6], d_params[7], d_params[8])
```

```python
import math

import jax
import jax.numpy as jnp
from jax import lax
from jax.sharding import PartitionSpec as P

EPSILON = 1e-05
BF = jnp.bfloat16
F32 = jnp.float32


def dot(a, b):
    return jnp.dot(a, b, preferred_element_type=F32)


def dot_t(a, b):
    return lax.dot_general(a, b, (((1,), (1,)), ((), ())), preferred_element_type=F32)


def t_dot(a, b):
    return lax.dot_general(a, b, (((0,), (0,)), ((), ())), preferred_element_type=F32)


def rotary(offsets, head_size):
    frequency = 10000.0 ** (-(jnp.arange(head_size // 2).astype(F32) * 2.0 / head_size))
    angles = offsets.astype(F32)[:, None] * frequency[None, :]
    return jnp.cos(angles), jnp.sin(angles)


def rotate(tensor, cosine, sine):
    middle = tensor.shape[-1] // 2
    a, b = tensor[..., :middle], tensor[..., middle:]
    return jnp.concatenate([a * cosine - b * sine, b * cosine + a * sine], -1)


def norm_back(source, factor, gain, incoming):
    scaled = incoming * gain
    grad_source = factor * scaled - source * factor**3 * jnp.mean(
        scaled * source, -1, keepdims=True
    )
    return grad_source, jnp.sum(incoming * source * factor, 0)


def to_rows(packed, n_ctx):
    rest = packed.shape[1:]
    v = packed.reshape((n_ctx, 2, -1) + rest)
    return jnp.concatenate([v[:, 0], v[::-1, 1]], 0).reshape((-1,) + rest)


def to_packed(rows, n_ctx):
    rest = rows.shape[1:]
    v = rows.reshape((2 * n_ctx, -1) + rest)
    return jnp.stack([v[:n_ctx], v[n_ctx:][::-1]], 1).reshape((-1,) + rest)


def local(
    acts,
    doc_lengths,
    w_query,
    w_key,
    w_value,
    w_out,
    w_gate,
    w_up,
    w_down,
    gain_attn,
    gain_mlp,
    cotangent,
):
    tok = acts.shape[2]
    width = acts.shape[3]
    n_ctx = lax.axis_size("ctx")
    me = lax.axis_index("ctx")
    row = n_ctx * tok
    head = w_query.shape[1]
    scale = 1.0 / math.sqrt(head)

    acts_rows = acts.reshape(tok, width)
    cot_low = cotangent.reshape(tok, width)
    gains = jnp.zeros((16, width), BF)
    gains = gains.at[0, :head].set(gain_attn).at[1, :head].set(gain_mlp)
    gathered = lax.all_gather(
        jnp.concatenate([acts_rows, gains], 0), "ctx", axis=0, tiled=False
    )
    cot_all = lax.all_gather(cot_low, "ctx", axis=0, tiled=True)
    tokens_all = gathered[:, :tok].reshape(row, width).astype(F32)
    gain_first = gathered[:, tok, :head].reshape(width).astype(F32)
    gain_second = gathered[:, tok + 1, :head].reshape(width).astype(F32)

    factor_all = lax.rsqrt(jnp.mean(tokens_all * tokens_all, -1, keepdims=True) + EPSILON)
    normed = (tokens_all * factor_all * gain_first).astype(BF)
    w_qkv = jnp.concatenate([w_query, w_key, w_value], 1)
    qkv = to_rows(dot(normed, w_qkv), n_ctx)

    lengths = doc_lengths.reshape(2)
    pos = jnp.arange(row, dtype=jnp.int32)
    doc = (pos >= lengths[0]).astype(jnp.int32)
    own = jnp.where(doc == 0, lengths[0], lengths[1])
    bias = -jnp.log(own.astype(F32))
    cosine, sine = rotary(pos - doc * lengths[0], head)
    visible = ((doc[None, :] == doc[:, None]) & (pos[None, :] <= pos[:, None])).astype(F32)

    q_rot = rotate(qkv[:, :head], cosine, sine).astype(BF)
    k_rot = rotate(qkv[:, head : 2 * head], cosine, sine).astype(BF)
    v_low = qkv[:, 2 * head :].astype(BF)
    score = dot_t(q_rot, k_rot) * scale + bias[:, None]
    sig = jax.nn.sigmoid(score)
    prob = (sig * visible).astype(BF)
    attended = to_packed(dot(prob, v_low).astype(BF), n_ctx)
    branch = lax.psum_scatter(
        dot(attended, w_out).astype(BF), "ctx", scatter_dimension=0, tiled=True
    ).astype(F32)

    tokens = acts_rows.astype(F32)
    factor_one = lax.rsqrt(jnp.mean(tokens * tokens, -1, keepdims=True) + EPSILON)
    residual = tokens + branch
    factor_two = lax.rsqrt(jnp.mean(residual * residual, -1, keepdims=True) + EPSILON)
    normed_two = (residual * factor_two * gain_second).astype(BF)
    normed_two_all = lax.all_gather(normed_two, "ctx", axis=0, tiled=True)

    gate = dot(normed_two_all, w_gate)
    up = dot(normed_two_all, w_up)
    d_hidden = dot_t(cot_all, w_down)
    sig_gate = jax.nn.sigmoid(gate)
    silu = gate * sig_gate
    hidden = (silu * up).astype(BF)
    d_gate = (d_hidden * up * sig_gate * (1.0 + gate * (1.0 - sig_gate))).astype(BF)
    d_up = (d_hidden * silu).astype(BF)
    d_normed_two = lax.psum_scatter(
        (dot_t(d_gate, w_gate) + dot_t(d_up, w_up)).astype(BF),
        "ctx",
        scatter_dimension=0,
        tiled=True,
    ).astype(F32)
    mlp_out = lax.psum_scatter(
        dot(hidden, w_down).astype(BF), "ctx", scatter_dimension=0, tiled=True
    ).astype(F32)
    mixed = (residual + mlp_out).astype(BF)
    grad_down = t_dot(hidden, cot_all)
    grad_gate = t_dot(normed_two_all, d_gate)
    grad_up = t_dot(normed_two_all, d_up)
    ff_totals = lax.psum(
        (grad_gate.astype(BF), grad_up.astype(BF), grad_down.astype(BF)), "grp"
    )

    d_from_two, gain_two_part = norm_back(residual, factor_two, gain_second, d_normed_two)
    d_residual = cot_low.astype(F32) + d_from_two
    d_branch = lax.all_gather(d_residual.astype(BF), "ctx", axis=0, tiled=True)
    grad_out = t_dot(attended, d_branch)
    d_attended = to_rows(dot_t(d_branch, w_out).astype(BF), n_ctx)

    d_prob = dot_t(d_attended, v_low)
    d_score = (d_prob * sig * (1.0 - sig) * visible).astype(BF)
    d_qrot = dot(d_score, k_rot) * scale
    d_krot = t_dot(d_score, q_rot) * scale
    d_vsum = t_dot(prob, d_attended)
    d_qkv = to_packed(
        jnp.concatenate(
            [rotate(d_qrot, cosine, -sine), rotate(d_krot, cosine, -sine), d_vsum], 1
        ).astype(BF),
        n_ctx,
    )
    grad_qkv = t_dot(normed, d_qkv)
    d_normed = lax.psum_scatter(
        dot_t(d_qkv, w_qkv).astype(BF), "ctx", scatter_dimension=0, tiled=True
    ).astype(F32)
    d_from_one, gain_one_part = norm_back(tokens, factor_one, gain_first, d_normed)
    acts_grad = d_residual + d_from_one

    attn_totals = lax.psum((grad_qkv.astype(BF), grad_out.astype(BF)), "grp")
    gain_parts = lax.psum(jnp.stack([gain_one_part, gain_two_part]), ("grp", "ctx"))
    gain_mine = lax.dynamic_slice_in_dim(gain_parts, me * head, head, 1)
    total_qkv = attn_totals[0].astype(F32)
    return (
        mixed.reshape(1, 1, tok, width),
        acts_grad.reshape(1, 1, tok, width),
        total_qkv[:, :head],
        total_qkv[:, head : 2 * head],
        total_qkv[:, 2 * head :],
        attn_totals[1].astype(F32),
        ff_totals[0].astype(F32),
        ff_totals[1].astype(F32),
        ff_totals[2].astype(F32),
        gain_mine[0],
        gain_mine[1],
    )


def solution(mesh):
    row = P("grp", "ctx", None, None)
    col = P(None, "ctx")
    dep = P("ctx", None)
    vec = P("ctx")
    in_specs = (row, P("grp", None), col, col, col, dep, col, col, dep, vec, vec, row)
    out_specs = (row, row, col, col, col, dep, col, col, dep, vec, vec)
    return jax.shard_map(local, mesh=mesh, in_specs=in_specs, out_specs=out_specs, check_vma=False)
```

```python
import math

import jax
import jax.numpy as jnp
from jax import lax
from jax.experimental import pallas as pl
from jax.experimental.pallas import tpu as pltpu
from jax.sharding import PartitionSpec as P

EPSILON = 1e-05
BF = jnp.bfloat16
F32 = jnp.float32
MESH = pl.DeviceIdType.MESH
VM = pl.BlockSpec(memory_space=pltpu.VMEM)
FF_ROWS = 352
FF_PAD = 384


def dot(a, b):
    return jnp.dot(a, b, preferred_element_type=F32)


def dot_t(a, b):
    return lax.dot_general(a, b, (((1,), (1,)), ((), ())), preferred_element_type=F32)


def t_dot(a, b):
    return lax.dot_general(a, b, (((0,), (0,)), ((), ())), preferred_element_type=F32)


def place():
    c, g = lax.axis_index("ctx"), lax.axis_index("grp")
    return c // 8, (c // 2) % 4, c % 2, g // 4, g % 4


def slot_at(pos, dz, dy, dk=0):
    z, y, k = pos[:3]
    return ((z + dz) % 2) * 8 + ((y + dy) % 4) * 2 + (k + dk) % 2


HOPS = {"p": (0, 1, 0), "m": (0, 3, 0), "z": (1, 0, 0), "c": (0, 0, 1)}
GROUP_HOPS = {"e": (0, 1), "w": (0, 3), "h": (1, 0)}


def neighbour(pos, link):
    if link in HOPS:
        return (lax.axis_index("grp"), slot_at(pos, *HOPS[link]))
    dh, dx = GROUP_HOPS[link]
    return (((pos[3] + dh) % 2) * 4 + (pos[4] + dx) % 4, lax.axis_index("ctx"))


def ctx_peer(d):
    return (lax.axis_index("grp"), (lax.axis_index("ctx") + d) % 16)


def grp_peer(d):
    return ((lax.axis_index("grp") + d) % 8, lax.axis_index("ctx"))


def greet(targets):
    barrier = pltpu.get_barrier_semaphore()
    for t in targets:
        pl.semaphore_signal(barrier, inc=1, device_id=t, device_id_type=MESH)
    pl.semaphore_wait(barrier, len(targets))


class Copies:
    def __init__(self, pos, send, recv):
        self.pos, self.send, self.recv, self.all = pos, send, recv, {}
        self.unsent, self.count = {}, 0

    def start(self, name, target, src, dst):
        n, self.count = self.count, self.count + 1
        if isinstance(target, str):
            target = neighbour(self.pos, target)
        copy = pltpu.make_async_remote_copy(
            src_ref=src,
            dst_ref=dst,
            send_sem=self.send.at[n],
            recv_sem=self.recv.at[n],
            device_id=target,
            device_id_type=MESH,
        )
        copy.start()
        self.all[name] = self.unsent[name] = copy

    def got(self, *names):
        for name in names:
            self.all[name].wait_recv()

    def sent(self, name):
        self.unsent.pop(name).wait_send()

    def finish(self):
        for name in list(self.unsent):
            self.sent(name)


def columns(width, body, step=512):
    def tile(j, _):
        body(pl.ds(pl.multiple_of(j * step, step), step))
        return 0

    lax.fori_loop(0, width // step, tile, 0)


def add_to(dst, *srcs):
    def tile(cols):
        total = dst[:, cols].astype(F32)
        for s in srcs:
            total = total + s[:, cols].astype(F32)
        dst[:, cols] = total.astype(dst.dtype)

    columns(dst.shape[1], tile)


N_GATHER = 35


def gather_steps(net, pos, buf, tag):
    def send(name, link, dz, dy, lo, n):
        ref = buf.at[slot_at(pos, dz, dy), pl.ds(lo, n)]
        net.start(tag + name, link, ref, ref)

    def got(*names):
        net.got(*[tag + name for name in names])

    send("p1", "p", 0, 0, 0, 128)
    send("m1", "m", 0, 0, 0, 128)
    send("z0", "z", 0, 0, 32, 64)
    send("c0", "c", 0, 0, 0, 128)
    send("zb00", "z", 0, 0, 0, 32)
    send("zb01", "z", 0, 0, 96, 32)
    got("c0")
    yield 0, 0
    got("p1")
    send("p2", "p", 0, 3, 0, 64)
    send("zb30", "z", 0, 3, 0, 32)
    send("zb31", "z", 0, 3, 96, 32)
    send("c1", "c", 0, 3, 0, 128)
    got("m1")
    send("m2", "m", 0, 1, 64, 64)
    send("zb10", "z", 0, 1, 0, 32)
    send("zb11", "z", 0, 1, 96, 32)
    send("c2", "c", 0, 1, 0, 128)
    got("z0")
    send("p3", "p", 1, 0, 32, 64)
    send("m3", "m", 1, 0, 32, 64)
    send("c3", "c", 1, 0, 32, 64)
    got("c1")
    yield 0, 3
    got("zb00", "zb01")
    send("c4", "c", 1, 0, 0, 32)
    send("c5", "c", 1, 0, 96, 32)
    got("c2")
    yield 0, 1
    got("p2")
    send("zb20", "z", 0, 2, 0, 32)
    send("c6", "c", 0, 2, 0, 64)
    got("m2")
    send("zb21", "z", 0, 2, 96, 32)
    send("c7", "c", 0, 2, 64, 64)
    got("c3", "c4", "c5")
    yield 1, 0
    got("p3")
    send("p4", "p", 1, 3, 32, 32)
    send("c8", "c", 1, 3, 32, 64)
    got("m3")
    send("m4", "m", 1, 1, 64, 32)
    send("c9", "c", 1, 1, 32, 64)
    got("c6", "c7")
    yield 0, 2
    got("zb30", "zb31")
    send("c10", "c", 1, 3, 0, 32)
    send("c11", "c", 1, 3, 96, 32)
    got("zb10", "zb11")
    send("c12", "c", 1, 1, 0, 32)
    send("c13", "c", 1, 1, 96, 32)
    got("c8", "c10", "c11")
    yield 1, 3
    got("p4")
    send("c14", "c", 1, 2, 32, 32)
    got("m4")
    send("c15", "c", 1, 2, 64, 32)
    got("zb20")
    send("c16", "c", 1, 2, 0, 32)
    got("zb21")
    send("c17", "c", 1, 2, 96, 32)
    got("c9", "c12", "c13")
    yield 1, 1
    got("c14", "c15", "c16", "c17")
    yield 1, 2


N_SCATTER = 25
INBOX_ROWS = 896


def scatter_scratch(w):
    return [
        pltpu.VMEM((16, 128, w), BF),
        pltpu.VMEM((8, 128, w), BF),
        pltpu.VMEM((INBOX_ROWS, w), BF),
    ]


class Scatter:
    def __init__(self, net, pos, part, sib, inbox, tag):
        self.net, self.pos, self.part, self.sib, self.tag = net, pos, part, sib, tag
        self.box, at = {}, 0
        for key, n in (
            [("zb%d%d" % (dy, h), 32) for dy in range(4) for h in range(2)]
            + [("p4", 32), ("m4", 32), ("p3", 64), ("m3", 64), ("p2", 64), ("m2", 64)]
            + [("p1", 128), ("m1", 128), ("z0", 64)]
        ):
            self.box[key] = inbox.at[pl.ds(at, n)]
            at += n

    def mine(self, dz, dy, lo=0, n=128):
        return self.part.at[slot_at(self.pos, dz, dy), pl.ds(lo, n)]

    def swap(self, dz, dy):
        src = self.part.at[slot_at(self.pos, dz, dy, 1)]
        self.net.start(self.tag + "c%d%d" % (dz, dy), "c", src, self.sib.at[dz * 4 + dy])

    def joined(self, dz, dy):
        self.got("c%d%d" % (dz, dy))
        add_to(self.mine(dz, dy), self.sib.at[dz * 4 + dy])

    def got(self, *names):
        self.net.got(*[self.tag + name for name in names])

    def put(self, name, link, src):
        self.net.start(self.tag + name, link, src, self.box[name])

    def put_zb(self, dy):
        for h, lo in ((0, 0), (1, 96)):
            self.put("zb%d%d" % (dy, h), "z", self.mine(1, dy, lo, 32))

    def take(self, name, dz, dy, lo, n):
        self.got(name)
        add_to(self.mine(dz, dy, lo, n), self.box[name])

    def take_zb(self, dy):
        self.take("zb%d0" % dy, 0, dy, 0, 32)
        self.take("zb%d1" % dy, 0, dy, 96, 32)

    def steps(self):
        self.joined(1, 2)
        self.put_zb(2)
        self.put("p4", "p", self.mine(1, 2, 64, 32))
        self.put("m4", "m", self.mine(1, 2, 32, 32))
        self.joined(1, 1)
        self.put_zb(1)
        self.joined(1, 3)
        self.put_zb(3)
        self.joined(1, 0)
        self.put_zb(0)
        self.joined(0, 2)
        yield
        self.take("p4", 1, 1, 64, 32)
        self.put("p3", "p", self.mine(1, 1, 32, 64))
        self.take("m4", 1, 3, 32, 32)
        self.put("m3", "m", self.mine(1, 3, 32, 64))
        self.joined(0, 1)
        self.joined(0, 3)
        yield
        self.take_zb(2)
        self.put("p2", "p", self.mine(0, 2, 64, 64))
        self.put("m2", "m", self.mine(0, 2, 0, 64))
        self.joined(0, 0)
        yield
        self.take("p3", 1, 0, 32, 64)
        self.take("m3", 1, 0, 32, 64)
        self.put("z0", "z", self.mine(1, 0, 32, 64))
        yield
        self.take_zb(1)
        self.take("p2", 0, 1, 64, 64)
        self.put("p1", "p", self.mine(0, 1))
        self.take_zb(3)
        self.take("m2", 0, 3, 0, 64)
        self.put("m1", "m", self.mine(0, 3))
        yield
        self.take_zb(0)
        self.take("z0", 0, 0, 32, 64)
        yield
        self.got("p1", "m1")

    def total(self, cols):
        sums = self.mine(0, 0)[:, cols].astype(F32)
        return sums + self.box["p1"][:, cols].astype(F32) + self.box["m1"][:, cols].astype(F32)


SCATTER_ORDER = [(1, 2), (1, 1), (1, 3), (1, 0), (0, 2), (0, 1), (0, 3), (0, 0)]


def pair_rows(pos, dz, dy):
    first = slot_at(pos, dz, dy) // 2
    return first * 2, pl.ds(pl.multiple_of(first * 256, 256), 256)


def product(pos, part, dz, dy, *factors):
    slot, rows = pair_rows(pos, dz, dy)

    def tile(cols):
        total = None
        for a, b in factors:
            term = dot(a[rows, :], b[:, cols])
            total = term if total is None else total + term
        part[slot, :, cols] = total[:128].astype(BF)
        part[slot + 1, :, cols] = total[128:].astype(BF)

    columns(part.shape[2], tile)


def quarter(pos, d, half=None):
    start = ((pos[4] + d) % 4) * 512
    if half is None:
        return pl.ds(pl.multiple_of(start, 512), 512)
    return pl.ds(pl.multiple_of(start + half * 256, 256), 256)


def ring_sum_scratch(rows):
    return [
        pltpu.VMEM((2, rows, 256), BF),
        pltpu.VMEM((3, rows, 512), BF),
    ]


N_RING_SUM = 5


def ring_sum_steps(net, pos, terms, chunk, far, near, tag):
    rows = terms.shape[0]
    net.start(tag + "e2", "e", terms.at[:, quarter(pos, 2, 0)], far.at[0])
    net.start(tag + "w2", "w", terms.at[:, quarter(pos, 2, 1)], far.at[1])
    yield
    for name, d, half in (("e", 1, 0), ("w", 3, 1)):
        net.got(tag + name + "2")

        def fold(i, _, d=d, half=half):
            r = pl.ds(pl.multiple_of(i * 32, 32), 32)
            cols = quarter(pos, d, half)
            terms[r, cols] = (terms[r, cols].astype(F32) + far[half, r, :].astype(F32)).astype(BF)
            return 0

        lax.fori_loop(0, rows // 32, fold, 0)
        net.start(tag + name + "1", name, terms.at[:, quarter(pos, d)], near.at[half])
    yield
    net.got(tag + "e1", tag + "w1")

    def join(i, _):
        r = pl.ds(pl.multiple_of(i * 32, 32), 32)
        total = terms[r, quarter(pos, 0)].astype(F32) + near[0, r, :].astype(F32)
        chunk[r, :] = (total + near[1, r, :].astype(F32)).astype(BF)
        return 0

    lax.fori_loop(0, rows // 32, join, 0)
    net.start(tag + "h", "h", chunk, near.at[2])
    yield
    net.got(tag + "h")
    net.sent(tag + "h")

    def across(i, _):
        r = pl.ds(pl.multiple_of(i * 32, 32), 32)
        chunk[r, :] = (chunk[r, :].astype(F32) + near[2, r, :].astype(F32)).astype(BF)
        return 0

    lax.fori_loop(0, rows // 32, across, 0)


N_RING_SHARE = 4


def ring_share_steps(net, pos, chunk, whole, tag):
    mine = quarter(pos, 0)
    net.start(tag + "e1", "e", chunk, whole.at[:, mine])
    net.start(tag + "w1", "w", chunk, whole.at[:, mine])
    whole[:, mine] = chunk[...]
    yield
    net.got(tag + "e1")
    ref = whole.at[:, quarter(pos, 3, 0)]
    net.start(tag + "e2", "e", ref, ref)
    net.got(tag + "w1")
    ref = whole.at[:, quarter(pos, 1, 1)]
    net.start(tag + "w2", "w", ref, ref)
    yield
    net.got(tag + "e2", tag + "w2")


def run(*steps):
    steps = list(steps)
    while steps:
        for s in list(steps):
            try:
                next(s)
            except StopIteration:
                steps.remove(s)


def sems(n):
    return [pltpu.SemaphoreType.DMA((n,)), pltpu.SemaphoreType.DMA((n,))]


def call(kernel, name, cid, outs, scratch, args, mib=60):
    return pl.pallas_call(
        kernel,
        out_shape=[jax.ShapeDtypeStruct(s, d) for s, d in outs],
        in_specs=[VM] * len(args),
        out_specs=[VM] * len(outs),
        scratch_shapes=scratch,
        compiler_params=pltpu.CompilerParams(
            collective_id=cid, has_side_effects=True, vmem_limit_bytes=mib * 2**20
        ),
        name=name,
    )(*args)


def norm_factor(u):
    return lax.rsqrt(jnp.mean(u * u, -1, keepdims=True) + EPSILON)


def acts_kernel(x, gains, out, gains_out, send, recv):
    pos = place()
    net = Copies(pos, send, recv)
    me = lax.axis_index("ctx")
    out[me] = x[...]
    gains_out[me] = gains[...]
    greet([ctx_peer(d) for d in range(1, 16)])
    for d in range(1, 16):
        ref = gains_out.at[me]
        net.start("g%d" % d, ctx_peer(d), ref, ref)
    for _ in gather_steps(net, pos, out, "x"):
        pass
    net.got(*["g%d" % d for d in range(1, 16)])
    net.finish()


def gather_acts(x, gains, cid):
    return call(
        acts_kernel,
        "gather_acts",
        cid,
        [((16, 128, 2048), BF), ((16, 16, 128), BF)],
        sems(N_GATHER + 15),
        [x, gains],
    )


def branch_kernel(a, w_out, cot, branch, cot_all, part, sib, inbox, send, recv):
    pos = place()
    net = Copies(pos, send, recv)
    cot_all[lax.axis_index("ctx")] = cot[...]
    greet([neighbour(pos, l) for l in "pmzc"])
    sums = Scatter(net, pos, part, sib, inbox, "s")
    for dz, dy in SCATTER_ORDER:
        product(pos, part, dz, dy, (a, w_out))
        sums.swap(dz, dy)
    run(sums.steps(), gather_steps(net, pos, cot_all, "x"))

    def last(cols):
        branch[:, cols] = sums.total(cols)

    columns(2048, last)
    net.finish()


def attention_branch(attended, w_out, cot, cid):
    return call(
        branch_kernel,
        "attention_branch",
        cid,
        [((128, 2048), F32), ((16, 128, 2048), BF)],
        scatter_scratch(2048) + sems(N_SCATTER + N_GATHER),
        [attended, w_out, cot],
    )


def mlp_kernel(
    acts,
    branch,
    gain,
    cot,
    w,
    residual,
    d_res,
    gain_part,
    hidden,
    grads,
    buf,
    low_t,
    part,
    sib,
    inbox,
    send,
    recv,
):
    pos = place()
    net = Copies(pos, send, recv)
    me = lax.axis_index("ctx")

    def normalise(i, _):
        r = pl.ds(pl.multiple_of(i * 32, 32), 32)
        u = acts[r, :].astype(F32) + branch[r, :]
        residual[r, :] = u
        buf[me, r, :] = (u * norm_factor(u) * gain[...]).astype(BF)
        return 0

    lax.fori_loop(0, 4, normalise, 0)
    greet([neighbour(pos, l) for l in "pmzc"])
    sums = Scatter(net, pos, part, sib, inbox, "s")
    for dz, dy in gather_steps(net, pos, buf, "x"):
        slot, rows = pair_rows(pos, dz, dy)
        n2 = buf[pl.ds(slot, 2)].reshape(256, 2048)
        ct = cot[pl.ds(slot, 2)].reshape(256, 2048)
        gate = dot_t(n2, w[0])
        up = dot_t(n2, w[1])
        d_hidden = dot_t(ct, w[2])
        sig = jax.nn.sigmoid(gate)
        silu = gate * sig
        h = (silu * up).astype(BF)
        dg = (d_hidden * up * sig * (1.0 + gate * (1.0 - sig))).astype(BF)
        du = (d_hidden * silu).astype(BF)
        hidden[rows, :] = h
        low_t[0, :, rows] = dg.T
        low_t[1, :, rows] = du.T
        low_t[2, :, rows] = h.T

        def tile(cols):
            t = dot(dg, w[0, :, cols]) + dot(du, w[1, :, cols])
            part[slot, :, cols] = t[:128].astype(BF)
            part[slot + 1, :, cols] = t[128:].astype(BF)

        columns(2048, tile)
        sums.swap(dz, dy)

    def weight_grads():
        for i, other in ((0, buf), (1, buf), (2, cot)):

            def tile(cols, i=i, other=other):
                rhs = other[:, :, cols].reshape(2048, 256)
                g = dot(low_t[i], rhs)
                grads[i * FF_ROWS : (i + 1) * FF_ROWS, cols] = g[:FF_ROWS].astype(BF)

            for half in range(2):

                def part_tile(j, _, half=half, tile=tile):
                    tile(pl.ds(pl.multiple_of(half * 1024 + j * 256, 256), 256))
                    return 0

                lax.fori_loop(0, 4, part_tile, 0)
                yield

    run(sums.steps(), weight_grads())

    gain_part[...] = jnp.zeros_like(gain_part)

    def back(i, _):
        r = pl.ds(pl.multiple_of(i * 32, 32), 32)
        slot = me
        e = (
            part[slot, r, :].astype(F32)
            + sums.box["p1"][r, :].astype(F32)
            + sums.box["m1"][r, :].astype(F32)
        )
        u = residual[r, :]
        f = norm_factor(u)
        scaled = e * gain[...]
        grad = f * scaled - u * f * f * f * jnp.mean(scaled * u, -1, keepdims=True)
        d_res[r, :] = cot[slot, r, :].astype(F32) + grad
        gain_part[...] += jnp.sum(e * u * f, 0, keepdims=True)
        return 0

    lax.fori_loop(0, 4, back, 0)
    net.finish()


def mlp(acts, branch, gain, cot_all, w, cid):
    return call(
        mlp_kernel,
        "mlp",
        cid,
        [
            ((128, 2048), F32),
            ((128, 2048), F32),
            ((1, 2048), F32),
            ((2048, FF_PAD), BF),
            ((3 * FF_ROWS, 2048), BF),
        ],
        [pltpu.VMEM((16, 128, 2048), BF), pltpu.VMEM((3, FF_PAD, 2048), BF)]
        + scatter_scratch(2048)
        + sems(N_SCATTER + N_GATHER),
        [acts, branch, gain, cot_all, w],
    )


def d_branch_kernel(
    d_res, attended, w_out, ff, d_att, grad_out, chunk, buf, total, far, near, send, recv
):
    pos = place()
    net = Copies(pos, send, recv)
    buf[lax.axis_index("ctx")] = d_res[...].astype(BF)
    total[...] = jnp.zeros_like(total)
    greet([neighbour(pos, l) for l in "pmzcewh"])

    def rows_in():
        for dz, dy in gather_steps(net, pos, buf, "x"):
            slot, rows = pair_rows(pos, dz, dy)
            d = buf[pl.ds(slot, 2)].reshape(256, 2048)
            d_att[rows, :] = dot_t(d, w_out[...]).astype(BF)
            total[...] += t_dot(attended[rows, :], d)
            yield

    run(ring_sum_steps(net, pos, ff, chunk, far, near, "r"), rows_in())
    grad_out[...] = total[...].astype(BF)
    net.finish()


def d_branch(d_res, attended, w_out, ff, cid):
    return call(
        d_branch_kernel,
        "d_branch",
        cid,
        [((2048, 128), BF), ((128, 2048), BF), ((3 * FF_ROWS, 512), BF)],
        [pltpu.VMEM((16, 128, 2048), BF), pltpu.VMEM((128, 2048), F32)]
        + ring_sum_scratch(3 * FF_ROWS)
        + sems(N_GATHER + N_RING_SUM),
        [d_res, attended, w_out, ff],
    )


def mixed_kernel(hidden, w, residual, chunk, mixed, whole, part, sib, inbox, send, recv):
    pos = place()
    net = Copies(pos, send, recv)
    greet([neighbour(pos, l) for l in "pmzcew"])
    sums = Scatter(net, pos, part, sib, inbox, "s")
    share = ring_share_steps(net, pos, chunk, whole, "r")
    next(share)
    for dz, dy in SCATTER_ORDER:
        product(pos, part, dz, dy, (hidden, w))
        sums.swap(dz, dy)
    run(sums.steps(), share)

    def last(cols):
        mixed[:, cols] = (residual[:, cols] + sums.total(cols)).astype(BF)

    columns(2048, last)
    net.finish()


def mlp_out(hidden, w_down, residual, chunk, cid):
    return call(
        mixed_kernel,
        "mlp_out",
        cid,
        [((128, 2048), BF), ((3 * FF_ROWS, 2048), BF)],
        scatter_scratch(2048) + sems(N_SCATTER + N_RING_SHARE),
        [hidden, w_down, residual, chunk],
    )


def d_normed_kernel(
    d_qkv,
    w,
    normed,
    acts,
    d_res,
    gain,
    grad_out,
    gain_two_part,
    acts_grad,
    whole,
    gains,
    part,
    sib,
    inbox,
    terms,
    chunk,
    far,
    near,
    low_t,
    gain_terms,
    gain_box,
    gain_sum,
    gain_wide,
    send,
    recv,
):
    pos = place()
    net = Copies(pos, send, recv)
    me = lax.axis_index("ctx")
    greet([ctx_peer(d) for d in range(1, 16)] + [grp_peer(d) for d in range(1, 8)])
    sums = Scatter(net, pos, part, sib, inbox, "s")
    low_t[...] = d_qkv[...].T
    terms[pl.ds(384, 128), :] = grad_out[...]
    gain_terms[...] = jnp.zeros_like(gain_terms)
    for j in range(16):
        cols = slice(j * 128, (j + 1) * 128)
        gain_terms[j, 0:1, :] = gain_two_part[:, cols]

    def weight_grads(d):
        for half in range(2):
            cols = quarter(pos, d, half)
            g = dot(low_t[...], normed[:, :, cols].reshape(2048, 256))
            terms[pl.ds(0, 384), cols] = g.astype(BF)
            by_column = jnp.sum(g * w[:, cols].astype(F32), 0, keepdims=True) / gain[:, cols]
            first = ((pos[4] + d) % 4) * 4 + half * 2
            gain_terms[first, 1:2, :] = by_column[:, :128]
            gain_terms[first + 1, 1:2, :] = by_column[:, 128:]

    def products(pairs):
        for dz, dy in pairs:
            product(pos, part, dz, dy, (d_qkv, w))
            sums.swap(dz, dy)

    weight_grads(2)
    ring = ring_sum_steps(net, pos, terms, chunk, far, near, "r")
    next(ring)
    products(SCATTER_ORDER[:4])
    back = sums.steps()
    weight_grads(1)
    products(SCATTER_ORDER[4:])
    next(back)
    weight_grads(3)
    weight_grads(0)
    next(back)
    next(ring)

    for d in range(1, 16):
        net.start("g%d" % d, ctx_peer(d), gain_terms.at[(me + d) % 16], gain_box.at[d])
    gain_box[0] = gain_terms[me]
    next(back)
    next(ring)
    net.got(*["g%d" % d for d in range(1, 16)])
    gain_sum[...] = jnp.sum(gain_box[...], 0)
    for d in range(1, 8):
        net.start("h%d" % d, grp_peer(d), gain_sum, gain_wide.at[d])
    gain_wide[0] = gain_sum[...]
    run(back, chain(ring, ring_share_steps(net, pos, chunk, whole, "q")))
    net.got(*["h%d" % d for d in range(1, 8)])
    gains[...] = jnp.sum(gain_wide[...], 0)

    def finish(i, _):
        r = pl.ds(pl.multiple_of(i * 32, 32), 32)
        e = (
            part[me, r, :].astype(F32)
            + sums.box["p1"][r, :].astype(F32)
            + sums.box["m1"][r, :].astype(F32)
        )
        u = acts[r, :].astype(F32)
        f = norm_factor(u)
        scaled = e * gain[...]
        grad = f * scaled - u * f * f * f * jnp.mean(scaled * u, -1, keepdims=True)
        acts_grad[r, :] = d_res[r, :] + grad
        return 0

    lax.fori_loop(0, 4, finish, 0)
    net.finish()


def chain(*steps):
    for s in steps:
        yield from s


def d_normed(d_qkv, w, normed, acts, d_res, gain, grad_out, gain_two_part, cid):
    return call(
        d_normed_kernel,
        "d_normed",
        cid,
        [((128, 2048), F32), ((512, 2048), BF), ((8, 128), F32)],
        scatter_scratch(2048)
        + [pltpu.VMEM((512, 2048), BF), pltpu.VMEM((512, 512), BF)]
        + ring_sum_scratch(512)
        + [
            pltpu.VMEM((384, 2048), BF),
            pltpu.VMEM((16, 8, 128), F32),
            pltpu.VMEM((16, 8, 128), F32),
            pltpu.VMEM((8, 128), F32),
            pltpu.VMEM((8, 8, 128), F32),
        ]
        + sems(N_SCATTER + N_RING_SUM + N_RING_SHARE + 22),
        [d_qkv, w, normed, acts, d_res, gain, grad_out, gain_two_part],
    )


def rotary(offsets, head_size):
    frequency = 10000.0 ** (-(jnp.arange(head_size // 2).astype(F32) * 2.0 / head_size))
    angles = offsets.astype(F32)[:, None] * frequency[None, :]
    return jnp.cos(angles), jnp.sin(angles)


def rotate(tensor, cosine, sine):
    middle = tensor.shape[-1] // 2
    a, b = tensor[..., :middle], tensor[..., middle:]
    return jnp.concatenate([a * cosine - b * sine, b * cosine + a * sine], -1)


def to_rows(packed, n_ctx):
    rest = packed.shape[1:]
    v = packed.reshape((n_ctx, 2, -1) + rest)
    return jnp.concatenate([v[:, 0], v[::-1, 1]], 0).reshape((-1,) + rest)


def to_packed(rows, n_ctx):
    rest = rows.shape[1:]
    v = rows.reshape((2 * n_ctx, -1) + rest)
    return jnp.stack([v[:n_ctx], v[n_ctx:][::-1]], 1).reshape((-1,) + rest)


def local(
    acts,
    doc_lengths,
    w_query,
    w_key,
    w_value,
    w_out,
    w_gate,
    w_up,
    w_down,
    gain_attn,
    gain_mlp,
    cotangent,
):
    tok = acts.shape[2]
    width = acts.shape[3]
    n_ctx = lax.axis_size("ctx")
    row = n_ctx * tok
    head = w_query.shape[1]
    ff = w_gate.shape[1]
    scale = 1.0 / math.sqrt(head)

    acts_rows = acts.reshape(tok, width)
    cot_low = cotangent.reshape(tok, width)
    gains = jnp.zeros((16, head), BF).at[0].set(gain_attn).at[1].set(gain_mlp)
    acts_all, gains_all = gather_acts(acts_rows, gains, 0)
    gain_first = gains_all[:, 0].reshape(1, width).astype(F32)
    gain_second = gains_all[:, 1].reshape(1, width).astype(F32)

    tokens_all = acts_all.reshape(row, width).astype(F32)
    normed = (tokens_all * norm_factor(tokens_all) * gain_first).astype(BF)
    w_qkv = jnp.concatenate([w_query, w_key, w_value], 1)
    qkv = to_rows(dot(normed, w_qkv), n_ctx)

    lengths = doc_lengths.reshape(2)
    pos = jnp.arange(row, dtype=jnp.int32)
    doc = (pos >= lengths[0]).astype(jnp.int32)
    own = jnp.where(doc == 0, lengths[0], lengths[1])
    bias = -jnp.log(own.astype(F32))
    cosine, sine = rotary(pos - doc * lengths[0], head)
    visible = ((doc[None, :] == doc[:, None]) & (pos[None, :] <= pos[:, None])).astype(F32)

    q_rot = rotate(qkv[:, :head], cosine, sine).astype(BF)
    k_rot = rotate(qkv[:, head : 2 * head], cosine, sine).astype(BF)
    v_low = qkv[:, 2 * head :].astype(BF)
    score = dot_t(q_rot, k_rot) * scale + bias[:, None]
    sig = jax.nn.sigmoid(score)
    prob = (sig * visible).astype(BF)
    attended = to_packed(dot(prob, v_low).astype(BF), n_ctx)
    branch, cot_all = attention_branch(attended, w_out, cot_low, 1)

    def padded(w):
        return jnp.pad(w, ((0, FF_PAD - ff), (0, 0)))

    ff_w = jnp.stack([padded(w_gate.T), padded(w_up.T), padded(w_down)])
    residual, d_res, gain_two_part, hidden, ff_grads = mlp(
        acts_rows, branch, gain_second, cot_all, ff_w, 2
    )
    d_att, grad_out, chunk = d_branch(d_res, attended, w_out, ff_grads, 3)
    mixed, ff_sums = mlp_out(hidden, ff_w[2], residual, chunk, 4)

    d_attended = to_rows(d_att, n_ctx)
    d_prob = dot_t(d_attended, v_low)
    d_score = (d_prob * sig * (1.0 - sig) * visible).astype(BF)
    d_qrot = dot(d_score, k_rot) * scale
    d_krot = t_dot(d_score, q_rot) * scale
    d_vsum = t_dot(prob, d_attended)
    d_qkv = to_packed(
        jnp.concatenate(
            [rotate(d_qrot, cosine, -sine), rotate(d_krot, cosine, -sine), d_vsum], 1
        ).astype(BF),
        n_ctx,
    )
    acts_grad, attn_sums, gain_grads = d_normed(
        d_qkv,
        w_qkv.T,
        normed.reshape(n_ctx, tok, width),
        acts_rows,
        d_res,
        gain_first,
        grad_out,
        gain_two_part,
        5,
    )

    def ff_grad(i):
        return ff_sums[i * FF_ROWS : i * FF_ROWS + ff].astype(F32)

    def attn_grad(i):
        return attn_sums[i * head : (i + 1) * head].astype(F32)

    return (
        mixed.reshape(1, 1, tok, width),
        acts_grad.reshape(1, 1, tok, width),
        attn_grad(0).T,
        attn_grad(1).T,
        attn_grad(2).T,
        attn_grad(3),
        ff_grad(0).T,
        ff_grad(1).T,
        ff_grad(2),
        gain_grads[1],
        gain_grads[0],
    )


def solution(mesh):
    row = P("grp", "ctx", None, None)
    col = P(None, "ctx")
    dep = P("ctx", None)
    vec = P("ctx")
    in_specs = (row, P("grp", None), col, col, col, dep, col, col, dep, vec, vec, row)
    out_specs = (row, row, col, col, col, dep, col, col, dep, vec, vec)
    return jax.shard_map(local, mesh=mesh, in_specs=in_specs, out_specs=out_specs, check_vma=False)
```

```python
import math

import jax
import jax.numpy as jnp
from jax import lax
from jax.experimental import pallas as pl
from jax.experimental.pallas import tpu as pltpu
from jax.sharding import PartitionSpec as P

EPSILON = 1e-05
BF = jnp.bfloat16
F32 = jnp.float32
MESH = pl.DeviceIdType.MESH
VM = pl.BlockSpec(memory_space=pltpu.VMEM)
FF_ROWS = 352
FF_PAD = 384


def dot(a, b):
    return jnp.dot(a, b, preferred_element_type=F32)


def dot_t(a, b):
    return lax.dot_general(a, b, (((1,), (1,)), ((), ())), preferred_element_type=F32)


def t_dot(a, b):
    return lax.dot_general(a, b, (((0,), (0,)), ((), ())), preferred_element_type=F32)


def place():
    c, g = lax.axis_index("ctx"), lax.axis_index("grp")
    return c // 8, (c // 2) % 4, c % 2, g // 4, g % 4


def slot_at(pos, dz, dy, dk=0):
    z, y, k = pos[:3]
    return ((z + dz) % 2) * 8 + ((y + dy) % 4) * 2 + (k + dk) % 2


HOPS = {"p": (0, 1, 0), "m": (0, 3, 0), "z": (1, 0, 0), "c": (0, 0, 1)}
GROUP_HOPS = {"e": (0, 1), "w": (0, 3), "h": (1, 0)}


def neighbour(pos, link):
    if link in HOPS:
        return (lax.axis_index("grp"), slot_at(pos, *HOPS[link]))
    dh, dx = GROUP_HOPS[link]
    return (((pos[3] + dh) % 2) * 4 + (pos[4] + dx) % 4, lax.axis_index("ctx"))


def ctx_peer(d):
    return (lax.axis_index("grp"), (lax.axis_index("ctx") + d) % 16)


def grp_peer(d):
    return ((lax.axis_index("grp") + d) % 8, lax.axis_index("ctx"))


def greet(targets):
    barrier = pltpu.get_barrier_semaphore()
    for t in targets:
        pl.semaphore_signal(barrier, inc=1, device_id=t, device_id_type=MESH)
    pl.semaphore_wait(barrier, len(targets))


class Copies:
    def __init__(self, pos, send, recv):
        self.pos, self.send, self.recv, self.all = pos, send, recv, {}
        self.unsent, self.count = {}, 0

    def start(self, name, target, src, dst):
        n, self.count = self.count, self.count + 1
        if isinstance(target, str):
            target = neighbour(self.pos, target)
        copy = pltpu.make_async_remote_copy(
            src_ref=src,
            dst_ref=dst,
            send_sem=self.send.at[n],
            recv_sem=self.recv.at[n],
            device_id=target,
            device_id_type=MESH,
        )
        copy.start()
        self.all[name] = self.unsent[name] = copy

    def got(self, *names):
        for name in names:
            self.all[name].wait_recv()

    def sent(self, name):
        self.unsent.pop(name).wait_send()

    def finish(self):
        for name in list(self.unsent):
            self.sent(name)


def columns(width, body, step=512):
    def tile(j, _):
        body(pl.ds(pl.multiple_of(j * step, step), step))
        return 0

    lax.fori_loop(0, width // step, tile, 0)


def add_to(dst, *srcs):
    def tile(cols):
        total = dst[:, cols].astype(F32)
        for s in srcs:
            total = total + s[:, cols].astype(F32)
        dst[:, cols] = total.astype(dst.dtype)

    columns(dst.shape[1], tile)


N_GATHER = 37


def gather_steps(net, pos, buf, tag):
    def send(name, link, dz, dy, lo, n):
        ref = buf.at[slot_at(pos, dz, dy), pl.ds(lo, n)]
        net.start(tag + name, link, ref, ref)

    def got(*names):
        net.got(*[tag + name for name in names])

    send("p1a", "p", 0, 0, 0, 64)
    send("m1a", "m", 0, 0, 64, 64)
    send("z0", "z", 0, 0, 32, 64)
    send("c0", "c", 0, 0, 0, 128)
    send("p1b", "p", 0, 0, 64, 64)
    send("m1b", "m", 0, 0, 0, 64)
    send("zb00", "z", 0, 0, 0, 32)
    send("zb01", "z", 0, 0, 96, 32)
    got("c0")
    yield 0, 0
    got("p1a")
    send("p2", "p", 0, 3, 0, 64)
    send("zb30", "z", 0, 3, 0, 32)
    got("m1a")
    send("m2", "m", 0, 1, 64, 64)
    send("zb11", "z", 0, 1, 96, 32)
    got("z0")
    send("p3", "p", 1, 0, 32, 64)
    send("m3", "m", 1, 0, 32, 64)
    send("c3", "c", 1, 0, 32, 64)
    yield None
    got("p1b")
    send("zb31", "z", 0, 3, 96, 32)
    send("c1", "c", 0, 3, 0, 128)
    got("m1b")
    send("zb10", "z", 0, 1, 0, 32)
    send("c2", "c", 0, 1, 0, 128)
    got("c1")
    yield 0, 3
    got("zb00", "zb01")
    send("c4", "c", 1, 0, 0, 32)
    send("c5", "c", 1, 0, 96, 32)
    got("c2")
    yield 0, 1
    got("p2")
    send("zb20", "z", 0, 2, 0, 32)
    send("c6", "c", 0, 2, 0, 64)
    got("m2")
    send("zb21", "z", 0, 2, 96, 32)
    send("c7", "c", 0, 2, 64, 64)
    got("c3", "c4", "c5")
    yield 1, 0
    got("p3")
    send("p4", "p", 1, 3, 32, 32)
    send("c8", "c", 1, 3, 32, 64)
    got("m3")
    send("m4", "m", 1, 1, 64, 32)
    send("c9", "c", 1, 1, 32, 64)
    got("c6", "c7")
    yield 0, 2
    got("zb30", "zb31")
    send("c10", "c", 1, 3, 0, 32)
    send("c11", "c", 1, 3, 96, 32)
    got("zb10", "zb11")
    send("c12", "c", 1, 1, 0, 32)
    send("c13", "c", 1, 1, 96, 32)
    got("c8", "c10", "c11")
    yield 1, 3
    got("p4")
    send("c14", "c", 1, 2, 32, 32)
    got("m4")
    send("c15", "c", 1, 2, 64, 32)
    got("c9", "c12", "c13")
    yield 1, 1
    got("zb20")
    send("c16", "c", 1, 2, 0, 32)
    got("zb21")
    send("c17", "c", 1, 2, 96, 32)
    got("c14", "c15", "c16", "c17")
    yield 1, 2


def gather_round_steps(net, pos, buf, tag):
    def send(name, link, dz, dy, lo=0, n=128):
        ref = buf.at[slot_at(pos, dz, dy), pl.ds(lo, n)]
        net.start(tag + name, link, ref, ref)

    def got(*names):
        net.got(*[tag + name for name in names])

    send("z0", "z", 0, 0)
    send("p1a", "p", 0, 0, 0, 64)
    send("m1a", "m", 0, 0, 64, 64)
    send("c0", "c", 0, 0)
    send("p1b", "p", 0, 0, 64, 64)
    send("m1b", "m", 0, 0, 0, 64)
    got("c0")
    yield 0, 0
    got("p1a")
    send("p2", "p", 0, 3, 0, 64)
    got("m1a")
    send("m2", "m", 0, 1, 64, 64)
    got("z0")
    send("p3a", "p", 1, 0, 0, 64)
    send("m3a", "m", 1, 0, 64, 64)
    send("p3b", "p", 1, 0, 64, 64)
    send("m3b", "m", 1, 0, 0, 64)
    send("c3", "c", 1, 0)
    got("p1b")
    send("c1", "c", 0, 3)
    got("m1b")
    send("c2", "c", 0, 1)
    got("c1")
    yield 0, 3
    got("c2")
    yield 0, 1
    got("p2")
    send("c4", "c", 0, 2, 0, 64)
    got("m2")
    send("c5", "c", 0, 2, 64, 64)
    got("c3")
    yield 1, 0
    got("p3a")
    send("p4", "p", 1, 3, 0, 64)
    got("m3a")
    send("m4", "m", 1, 1, 64, 64)
    got("c4", "c5")
    yield 0, 2
    got("p3b")
    send("c6", "c", 1, 3)
    got("m3b")
    send("c7", "c", 1, 1)
    got("c6")
    yield 1, 3
    got("c7")
    yield 1, 1
    got("p4")
    send("c8", "c", 1, 2, 0, 64)
    got("m4")
    send("c9", "c", 1, 2, 64, 64)
    got("c8", "c9")
    yield 1, 2


N_SCATTER = 29
INBOX_ROWS = 896


def scatter_scratch(w):
    return [
        pltpu.VMEM((16, 128, w), BF),
        pltpu.VMEM((8, 128, w), BF),
        pltpu.VMEM((INBOX_ROWS, w), BF),
    ]


class Scatter:
    def __init__(self, net, pos, part, sib, inbox, tag, z_last=False):
        self.net, self.pos, self.part, self.sib, self.tag = net, pos, part, sib, tag
        self.box, at = {}, 0
        if z_last:
            rows = [(side + step, n) for step, n in zip("4321", (64, 128, 64, 128)) for side in "pm"]
            rows.append(("z0", 128))
        else:
            rows = [("zb%d%d" % (dy, h), 32) for dy in range(4) for h in range(2)]
            rows += [(side + step, n) for step, n in zip("4321", (32, 64, 64, 128)) for side in "pm"]
            rows.append(("z0", 64))
        for key, n in rows:
            self.box[key] = inbox.at[pl.ds(at, n)]
            at += n
        for side in "pm":
            whole = self.box[side + "1"]
            self.box[side + "1a"] = whole.at[pl.ds(32, 64)]
            self.box[side + "1b"] = whole.at[pl.ds(0, 32)]
            self.box[side + "1c"] = whole.at[pl.ds(96, 32)]

    def mine(self, dz, dy, lo=0, n=128):
        return self.part.at[slot_at(self.pos, dz, dy), pl.ds(lo, n)]

    def swap(self, dz, dy):
        src = self.part.at[slot_at(self.pos, dz, dy, 1)]
        self.net.start(self.tag + "c%d%d" % (dz, dy), "c", src, self.sib.at[dz * 4 + dy])

    def joined(self, dz, dy):
        self.got("c%d%d" % (dz, dy))
        add_to(self.mine(dz, dy), self.sib.at[dz * 4 + dy])

    def got(self, *names):
        self.net.got(*[self.tag + name for name in names])

    def put(self, name, link, src):
        self.net.start(self.tag + name, link, src, self.box[name])

    def put_zb(self, dy):
        for h, lo in ((0, 0), (1, 96)):
            self.put("zb%d%d" % (dy, h), "z", self.mine(1, dy, lo, 32))

    def take(self, name, dz, dy, lo, n):
        self.got(name)
        add_to(self.mine(dz, dy, lo, n), self.box[name])

    def take_zb(self, dy):
        self.take("zb%d0" % dy, 0, dy, 0, 32)
        self.take("zb%d1" % dy, 0, dy, 96, 32)

    def steps(self):
        self.joined(1, 2)
        self.put_zb(2)
        self.put("p4", "p", self.mine(1, 2, 64, 32))
        self.put("m4", "m", self.mine(1, 2, 32, 32))
        self.joined(1, 1)
        self.put_zb(1)
        self.joined(1, 3)
        self.put_zb(3)
        yield
        self.take("p4", 1, 1, 64, 32)
        self.put("p3", "p", self.mine(1, 1, 32, 64))
        self.take("m4", 1, 3, 32, 32)
        self.put("m3", "m", self.mine(1, 3, 32, 64))
        self.joined(0, 2)
        yield
        self.take_zb(2)
        self.put("p2", "p", self.mine(0, 2, 64, 64))
        self.put("m2", "m", self.mine(0, 2, 0, 64))
        self.joined(1, 0)
        self.joined(0, 1)
        self.joined(0, 3)
        yield
        self.take("p3", 1, 0, 32, 64)
        self.take("m3", 1, 0, 32, 64)
        self.put("z0", "z", self.mine(1, 0, 32, 64))
        yield
        self.take("p2", 0, 1, 64, 64)
        self.put("p1a", "p", self.mine(0, 1, 32, 64))
        self.take("m2", 0, 3, 0, 64)
        self.put("m1a", "m", self.mine(0, 3, 32, 64))
        self.joined(0, 0)
        yield
        self.take_zb(1)
        self.put("p1b", "p", self.mine(0, 1, 0, 32))
        self.put("p1c", "p", self.mine(0, 1, 96, 32))
        self.put_zb(0)
        self.take_zb(3)
        self.put("m1b", "m", self.mine(0, 3, 0, 32))
        self.put("m1c", "m", self.mine(0, 3, 96, 32))
        yield
        self.take("z0", 0, 0, 32, 64)
        self.take_zb(0)
        yield
        self.got("p1a", "m1a", "p1b", "p1c", "m1b", "m1c")

    def z_last_steps(self):
        self.joined(1, 2)
        self.put("p4", "p", self.mine(1, 2, 64, 64))
        self.put("m4", "m", self.mine(1, 2, 0, 64))
        self.joined(0, 2)
        self.put("p2", "p", self.mine(0, 2, 64, 64))
        self.put("m2", "m", self.mine(0, 2, 0, 64))
        self.joined(1, 1)
        self.joined(1, 3)
        yield
        self.take("p4", 1, 1, 64, 64)
        self.put("p3", "p", self.mine(1, 1))
        self.take("m4", 1, 3, 0, 64)
        self.put("m3", "m", self.mine(1, 3))
        self.joined(0, 1)
        self.joined(0, 3)
        yield
        self.take("p2", 0, 1, 64, 64)
        self.put("p1", "p", self.mine(0, 1))
        self.take("m2", 0, 3, 0, 64)
        self.put("m1", "m", self.mine(0, 3))
        self.joined(1, 0)
        self.joined(0, 0)
        yield
        self.take("p3", 1, 0, 0, 128)
        self.take("m3", 1, 0, 0, 128)
        self.put("z0", "z", self.mine(1, 0))
        yield
        self.take("z0", 0, 0, 0, 128)
        self.got("p1", "m1")

    def total(self, cols):
        sums = self.mine(0, 0)[:, cols].astype(F32)
        return sums + self.box["p1"][:, cols].astype(F32) + self.box["m1"][:, cols].astype(F32)


SCATTER_ORDER = [(1, 2), (1, 1), (1, 3), (1, 0), (0, 2), (0, 1), (0, 3), (0, 0)]


def pair_rows(pos, dz, dy):
    first = slot_at(pos, dz, dy) // 2
    return first * 2, pl.ds(pl.multiple_of(first * 256, 256), 256)


def product(pos, part, dz, dy, *factors):
    slot, rows = pair_rows(pos, dz, dy)

    def tile(cols):
        total = None
        for a, b in factors:
            term = dot(a[rows, :], b[:, cols])
            total = term if total is None else total + term
        part[slot, :, cols] = total[:128].astype(BF)
        part[slot + 1, :, cols] = total[128:].astype(BF)

    columns(part.shape[2], tile)


def span(pos, d, part, half=None):
    start = ((pos[4] + d) % 4) * 512 + part * 256
    if half is None:
        return pl.ds(pl.multiple_of(start, 256), 256)
    return pl.ds(pl.multiple_of(start + half * 128, 128), 128)


def ring_sum_scratch(rows):
    return [
        pltpu.VMEM((2, 2, rows, 128), BF),
        pltpu.VMEM((2, 2, rows, 256), BF),
    ]


def by_rows(rows, body):
    def step(i, _):
        body(pl.ds(pl.multiple_of(i * 32, 32), 32))
        return 0

    lax.fori_loop(0, rows // 32, step, 0)


class Ring:
    def __init__(self, net, pos, tag):
        self.net, self.pos, self.tag = net, pos, tag

    def put(self, name, link, src, dst):
        self.net.start(self.tag + name, link, src, dst)

    def got(self, *names):
        self.net.got(*[self.tag + name for name in names])

    def far(self, p, terms, far):
        self.put("e2%d" % p, "e", terms.at[:, span(self.pos, 2, p, 0)], far.at[p, 0])
        self.put("w2%d" % p, "w", terms.at[:, span(self.pos, 2, p, 1)], far.at[p, 1])

    def near(self, p, terms, far, near):
        for name, d, half in (("e", 1, 0), ("w", 3, 1)):
            self.got("%s2%d" % (name, p))
            cols = span(self.pos, d, p, half)

            def fold(r, half=half, cols=cols):
                total = terms[r, cols].astype(F32) + far[p, half, r, :].astype(F32)
                terms[r, cols] = total.astype(BF)

            by_rows(terms.shape[0], fold)
            src = terms.at[:, span(self.pos, d, p)]
            self.put("%s1%d" % (name, p), name, src, near.at[p, half])

    def join(self, p, terms, near, chunk):
        self.got("e1%d" % p, "w1%d" % p)

        def add(r):
            total = terms[r, span(self.pos, 0, p)].astype(F32) + near[p, 0, r, :].astype(F32)
            chunk[p, r, :] = (total + near[p, 1, r, :].astype(F32)).astype(BF)

        by_rows(terms.shape[0], add)

    def across(self, p, chunk, box):
        self.put("h%d" % p, "h", chunk.at[p], box.at[p])

    def crossed(self, p, chunk, box, whole):
        self.got("h%d" % p)
        cols = span(self.pos, 0, p)

        def add(r):
            total = chunk[p, r, :].astype(F32) + box[p, r, :].astype(F32)
            whole[r, cols] = total.astype(BF)

        by_rows(whole.shape[0], add)
        for name in "ew":
            self.put("%s3%d" % (name, p), name, whole.at[:, cols], whole.at[:, cols])

    def share(self, p, whole):
        for name, d, half in (("e", 3, 0), ("w", 1, 1)):
            self.got("%s3%d" % (name, p))
            ref = whole.at[:, span(self.pos, d, p, half)]
            self.put("%s4%d" % (name, p), name, ref, ref)

    def shared(self, p):
        self.got("e4%d" % p, "w4%d" % p)


N_RING_SUM = 8
N_RING_SHARE = 10


def run(*steps):
    steps = list(steps)
    while steps:
        for s in list(steps):
            try:
                next(s)
            except StopIteration:
                steps.remove(s)


def sems(n):
    return [pltpu.SemaphoreType.DMA((n,)), pltpu.SemaphoreType.DMA((n,))]


def call(kernel, name, cid, outs, scratch, args, mib=60):
    return pl.pallas_call(
        kernel,
        out_shape=[jax.ShapeDtypeStruct(s, d) for s, d in outs],
        in_specs=[VM] * len(args),
        out_specs=[VM] * len(outs),
        scratch_shapes=scratch,
        compiler_params=pltpu.CompilerParams(
            collective_id=cid, has_side_effects=True, vmem_limit_bytes=mib * 2**20
        ),
        name=name,
    )(*args)


def norm_factor(u):
    return lax.rsqrt(jnp.mean(u * u, -1, keepdims=True) + EPSILON)


def d_normed_kernel(
    d_qkv,
    w,
    normed,
    acts,
    d_res,
    gain,
    grad_out,
    gain_two_part,
    acts_grad,
    whole,
    gains,
    part,
    sib,
    inbox,
    terms,
    chunk,
    box,
    far,
    near,
    low_t,
    gain_terms,
    gain_box,
    gain_sum,
    gain_wide,
    send,
    recv,
):
    pos = place()
    net = Copies(pos, send, recv)
    me = lax.axis_index("ctx")
    greet([ctx_peer(d) for d in range(1, 16)] + [grp_peer(d) for d in range(1, 8)])
    sums = Scatter(net, pos, part, sib, inbox, "s", True)
    low_t[...] = d_qkv[...].T
    terms[pl.ds(384, 128), :] = grad_out[...]
    gain_terms[...] = jnp.zeros_like(gain_terms)
    for j in range(16):
        cols = slice(j * 128, (j + 1) * 128)
        gain_terms[j, 0:1, :] = gain_two_part[:, cols]

    def weight_grads(d, p):
        cols = span(pos, d, p)
        g = dot(low_t[...], normed[:, :, cols].reshape(2048, 256))
        terms[pl.ds(0, 384), cols] = g.astype(BF)
        by_column = jnp.sum(g * w[:, cols].astype(F32), 0, keepdims=True) / gain[:, cols]
        first = ((pos[4] + d) % 4) * 4 + p * 2
        gain_terms[first, 1:2, :] = by_column[:, :128]
        gain_terms[first + 1, 1:2, :] = by_column[:, 128:]

    def products(pairs):
        for dz, dy in pairs:
            product(pos, part, dz, dy, (d_qkv, w))
            sums.swap(dz, dy)

    ring = Ring(net, pos, "r")
    back = sums.z_last_steps()
    weight_grads(2, 0)
    ring.far(0, terms, far)
    products(SCATTER_ORDER[:1])
    weight_grads(2, 1)
    ring.far(1, terms, far)
    products(SCATTER_ORDER[1:])
    next(back)
    weight_grads(1, 0)
    weight_grads(3, 0)
    ring.near(0, terms, far, near)
    next(back)
    weight_grads(1, 1)
    weight_grads(3, 1)
    ring.near(1, terms, far, near)
    next(back)
    weight_grads(0, 0)
    weight_grads(0, 1)
    for d in range(1, 16):
        net.start("g%d" % d, ctx_peer(d), gain_terms.at[(me + d) % 16], gain_box.at[d])
    gain_box[0] = gain_terms[me]
    ring.join(0, terms, near, chunk)
    ring.across(0, chunk, box)
    ring.join(1, terms, near, chunk)
    ring.across(1, chunk, box)
    next(back)
    ring.crossed(0, chunk, box, whole)
    net.got(*["g%d" % d for d in range(1, 16)])
    gain_sum[...] = jnp.sum(gain_box[...], 0)
    for d in range(1, 8):
        net.start("h%d" % d, grp_peer(d), gain_sum, gain_wide.at[d])
    gain_wide[0] = gain_sum[...]
    ring.crossed(1, chunk, box, whole)
    ring.share(0, whole)
    run(back)
    ring.share(1, whole)
    net.got(*["h%d" % d for d in range(1, 8)])
    gains[...] = jnp.sum(gain_wide[...], 0)

    def finish(i, _):
        r = pl.ds(pl.multiple_of(i * 32, 32), 32)
        e = (
            part[me, r, :].astype(F32)
            + sums.box["p1"][r, :].astype(F32)
            + sums.box["m1"][r, :].astype(F32)
        )
        u = acts[r, :].astype(F32)
        f = norm_factor(u)
        scaled = e * gain[...]
        grad = f * scaled - u * f * f * f * jnp.mean(scaled * u, -1, keepdims=True)
        acts_grad[r, :] = d_res[r, :] + grad
        return 0

    lax.fori_loop(0, 4, finish, 0)
    ring.shared(0)
    ring.shared(1)
    net.finish()


def d_normed(d_qkv, w, normed, acts, d_res, gain, grad_out, gain_two_part, cid):
    return call(
        d_normed_kernel,
        "d_normed",
        cid,
        [((128, 2048), F32), ((512, 2048), BF), ((8, 128), F32)],
        scatter_scratch(2048)
        + [pltpu.VMEM((512, 2048), BF), pltpu.VMEM((2, 512, 256), BF), pltpu.VMEM((2, 512, 256), BF)]
        + ring_sum_scratch(512)
        + [
            pltpu.VMEM((384, 2048), BF),
            pltpu.VMEM((16, 8, 128), F32),
            pltpu.VMEM((16, 8, 128), F32),
            pltpu.VMEM((8, 128), F32),
            pltpu.VMEM((8, 8, 128), F32),
        ]
        + sems(N_SCATTER + N_RING_SUM + N_RING_SHARE + 22),
        [d_qkv, w, normed, acts, d_res, gain, grad_out, gain_two_part],
    )


def rope(u, cosine, sine):
    return u * cosine + pltpu.roll(u, 64, 1) * sine


def block_start(c, half):
    return c * 64 if half == 0 else (31 - c) * 64


def document_start(position, lens):
    first = lens[0:1, 0:1]
    return jnp.where(position >= first, first, 0)


def bias_at(position, lens):
    own = jnp.where(position >= lens[0:1, 0:1], lens[1:2, 0:1], lens[0:1, 0:1])
    return -jnp.log(own.astype(F32))


def project_kernel(
    x,
    gains,
    lens,
    frequency,
    w_query,
    w_key,
    w_value,
    normed,
    qkv,
    cosines,
    sines,
    gain_rows,
    buf,
    gain_box,
    w,
    send,
    recv,
):
    pos = place()
    net = Copies(pos, send, recv)
    me = lax.axis_index("ctx")
    buf[me] = x[...]
    gain_box[me] = gains[...]
    greet([ctx_peer(d) for d in range(1, 16)])
    for d in range(1, 16):
        ref = gain_box.at[me]
        net.start("g%d" % d, ctx_peer(d), ref, ref)
    arrivals = gather_steps(net, pos, buf, "x")
    dz, dy = next(arrivals)

    def table(i, _):
        r = pl.ds(pl.multiple_of(i * 256, 256), 256)
        position = lax.broadcasted_iota(jnp.int32, (256, 128), 0) + i * 256
        offset = position - document_start(position, lens)
        angle = offset.astype(F32) * frequency[0:1, :]
        lane = lax.broadcasted_iota(jnp.int32, (256, 128), 1)
        cosines[r, :] = jnp.cos(angle)
        sines[r, :] = jnp.where(lane < 64, -1.0, 1.0) * jnp.sin(angle)
        return 0

    lax.fori_loop(0, 8, table, 0)
    for i, ref in enumerate((w_query, w_key, w_value)):
        w[:, i * 128 : (i + 1) * 128] = ref[...]
    net.got(*["g%d" % d for d in range(1, 16)])
    gain_rows[...] = jnp.zeros_like(gain_rows)
    for j in range(16):
        gain_rows[0:2, j * 128 : (j + 1) * 128] = gain_box[j].astype(F32)[0:2]

    while True:
        slot, _ = pair_rows(pos, dz, dy)

        def normalise(i, _, slot=slot):
            r = pl.ds(pl.multiple_of((i % 2) * 64, 64), 64)
            u = buf[slot + i // 2, r, :].astype(F32)
            normed[slot + i // 2, r, :] = (u * norm_factor(u) * gain_rows[0:1, :]).astype(BF)
            return 0

        lax.fori_loop(0, 4, normalise, 0)
        out = dot(normed[pl.ds(slot, 2)].reshape(256, 2048), w[...])
        for b in range(2):
            for half in range(2):
                at = pl.ds(pl.multiple_of(block_start(slot + b, half), 64), 64)
                rows = slice(b * 128 + half * 64, b * 128 + half * 64 + 64)
                c, s = cosines[at, :], sines[at, :]
                qkv[0, at, :] = rope(out[rows, :128], c, s).astype(BF)
                qkv[1, at, :] = rope(out[rows, 128:256], c, s).astype(BF)
                qkv[2, at, :] = out[rows, 256:].astype(BF)
        arrived = next(arrivals, ())
        if arrived is None:
            arrived = next(arrivals)
        if not arrived:
            break
        dz, dy = arrived
    net.finish()


def project(x, gains, lens, frequency, w_query, w_key, w_value, cid):
    return call(
        project_kernel,
        "project",
        cid,
        [
            ((16, 128, 2048), BF),
            ((3, 2048, 128), BF),
            ((2048, 128), F32),
            ((2048, 128), F32),
            ((8, 2048), F32),
        ],
        [
            pltpu.VMEM((16, 128, 2048), BF),
            pltpu.VMEM((16, 16, 128), BF),
            pltpu.VMEM((2048, 384), BF),
        ]
        + sems(N_GATHER + 15),
        [x, gains, lens, frequency, w_query, w_key, w_value],
    )


SCALE = 1.0 / math.sqrt(128)


def attend_block(qkv, lens, i):
    q = qkv[0, 256 * i : 256 * (i + 1), :]
    row = lax.broadcasted_iota(jnp.int32, (256, 1), 0) + 256 * i
    start = document_start(row, lens)
    bias = bias_at(row, lens)
    total = jnp.zeros((256, 128), F32)
    for lo in range(0, 256 * (i + 1), 512):
        n = min(512, 256 * (i + 1) - lo)
        score = dot_t(q, qkv[1, lo : lo + n, :]) * SCALE + bias
        col = lax.broadcasted_iota(jnp.int32, (1, n), 1) + lo
        visible = col >= start
        if lo + n > 256 * i:
            visible = visible & (col <= row)
        prob = jnp.where(visible, jax.nn.sigmoid(score), 0.0).astype(BF)
        total = total + dot(prob, qkv[2, lo : lo + n, :])
    return total


def packed_start(block):
    return block * 128 if block < 16 else (31 - block) * 128 + 64


def middle_kernel(
    qkv,
    lens,
    w_out,
    cot,
    acts,
    gain,
    w,
    attended,
    residual,
    d_res,
    gain_part,
    hidden,
    grads,
    cot_all,
    buf,
    low_t,
    part,
    sib,
    inbox,
    send,
    recv,
):
    pos = place()
    net = Copies(pos, send, recv)
    me = lax.axis_index("ctx")
    cot_all[me] = cot[...]
    greet([neighbour(pos, l) for l in "pmzc"])
    cots = gather_steps(net, pos, cot_all, "c")
    next(cots)
    for i in range(8):
        out = attend_block(qkv, lens, i).astype(BF)
        for b in range(4):
            at = packed_start(4 * i + b)
            attended[at : at + 64, :] = out[64 * b : 64 * (b + 1)]
        if i == 6:
            next(cots)
    sums = Scatter(net, pos, part, sib, inbox, "a")
    for dz, dy in SCATTER_ORDER:
        product(pos, part, dz, dy, (attended, w_out))
        sums.swap(dz, dy)
    run(sums.steps(), cots)

    def normalise(i, _):
        r = pl.ds(pl.multiple_of(i * 32, 32), 32)
        u = (
            acts[r, :].astype(F32)
            + part[me, r, :].astype(F32)
            + sums.box["p1"][r, :].astype(F32)
            + sums.box["m1"][r, :].astype(F32)
        )
        residual[r, :] = u
        buf[me, r, :] = (u * norm_factor(u) * gain[...]).astype(BF)
        return 0

    lax.fori_loop(0, 4, normalise, 0)
    net.finish()
    sums = Scatter(net, pos, part, sib, inbox, "s")
    for arrived in gather_steps(net, pos, buf, "x"):
        if arrived is None:
            continue
        dz, dy = arrived
        slot, rows = pair_rows(pos, dz, dy)
        n2 = buf[pl.ds(slot, 2)].reshape(256, 2048)
        ct = cot_all[pl.ds(slot, 2)].reshape(256, 2048)
        gate = dot_t(n2, w[0])
        up = dot_t(n2, w[1])
        d_hidden = dot_t(ct, w[2])
        sig = jax.nn.sigmoid(gate)
        silu = gate * sig
        h = (silu * up).astype(BF)
        dg = (d_hidden * up * sig * (1.0 + gate * (1.0 - sig))).astype(BF)
        du = (d_hidden * silu).astype(BF)
        hidden[rows, :] = h
        low_t[0, :, rows] = dg.T
        low_t[1, :, rows] = du.T
        low_t[2, :, rows] = h.T

        def tile(cols):
            t = dot(dg, w[0, :, cols]) + dot(du, w[1, :, cols])
            part[slot, :, cols] = t[:128].astype(BF)
            part[slot + 1, :, cols] = t[128:].astype(BF)

        columns(2048, tile)
        sums.swap(dz, dy)

    def weight_grads():
        for i, other in ((0, buf), (1, buf), (2, cot_all)):

            def tile(cols, i=i, other=other):
                rhs = other[:, :, cols].reshape(2048, 256)
                g = dot(low_t[i], rhs)
                grads[i * FF_ROWS : (i + 1) * FF_ROWS, cols] = g[:FF_ROWS].astype(BF)

            for half in range(2):

                def part_tile(j, _, half=half, tile=tile):
                    tile(pl.ds(pl.multiple_of(half * 1024 + j * 256, 256), 256))
                    return 0

                lax.fori_loop(0, 4, part_tile, 0)
                yield

    run(sums.steps(), weight_grads())

    gain_part[...] = jnp.zeros_like(gain_part)

    def back(i, _):
        r = pl.ds(pl.multiple_of(i * 32, 32), 32)
        slot = me
        e = (
            part[slot, r, :].astype(F32)
            + sums.box["p1"][r, :].astype(F32)
            + sums.box["m1"][r, :].astype(F32)
        )
        u = residual[r, :]
        f = norm_factor(u)
        scaled = e * gain[...]
        grad = f * scaled - u * f * f * f * jnp.mean(scaled * u, -1, keepdims=True)
        d_res[r, :] = cot[r, :].astype(F32) + grad
        gain_part[...] += jnp.sum(e * u * f, 0, keepdims=True)
        return 0

    lax.fori_loop(0, 4, back, 0)
    net.finish()


def middle(*args):
    return call(
        middle_kernel,
        "middle",
        1,
        [
            ((2048, 128), BF),
            ((128, 2048), F32),
            ((128, 2048), F32),
            ((1, 2048), F32),
            ((2048, FF_PAD), BF),
            ((3 * FF_ROWS, 2048), BF),
        ],
        [pltpu.VMEM((16, 128, 2048), BF), pltpu.VMEM((16, 128, 2048), BF)]
        + [pltpu.VMEM((3, FF_PAD, 2048), BF)]
        + scatter_scratch(2048)
        + sems(2 * N_SCATTER + 2 * N_GATHER),
        args,
        62,
    )


def attention_back_kernel(
    d_res,
    attended,
    w_out,
    ff,
    qkv,
    lens,
    cosines,
    sines,
    hidden,
    w_down,
    residual,
    d_qkv,
    grad_out,
    mixed,
    whole,
    buf,
    part,
    sib,
    inbox,
    far,
    near,
    chunk,
    box,
    total,
    do,
    dq,
    send,
    recv,
):
    pos = place()
    net = Copies(pos, send, recv)
    buf[lax.axis_index("ctx")] = d_res[...].astype(BF)
    greet([neighbour(pos, l) for l in "pmzcewh"])
    sums = Scatter(net, pos, part, sib, inbox, "s", True)
    back = sums.z_last_steps()
    ring = Ring(net, pos, "r")
    arrivals = gather_steps(net, pos, buf, "x")

    def arrive():
        pair = next(arrivals)
        if pair is None:
            pair = next(arrivals)
        slot, rows = pair_rows(pos, *pair)
        d = buf[pl.ds(slot, 2)].reshape(256, 2048)
        g = dot_t(d, w_out[...]).astype(BF)
        for b in range(2):
            for half in range(2):
                at = pl.ds(pl.multiple_of(block_start(slot + b, half), 64), 64)
                do[at, :] = g[b * 128 + half * 64 : b * 128 + half * 64 + 64]
        total[...] += t_dot(attended[rows, :], d)

    def products(pairs):
        for dz, dy in pairs:
            product(pos, part, dz, dy, (hidden, w_down))
            sums.swap(dz, dy)

    def put(block, value, i):
        for b in range(4):
            at = packed_start(4 * block + b)
            d_qkv[at : at + 64, 128 * i : 128 * (i + 1)] = value[64 * b : 64 * (b + 1)]

    def unrotate(u, block):
        r = slice(256 * block, 256 * (block + 1))
        return rope(u * SCALE, cosines[r, :], -sines[r, :]).astype(BF)

    def keys(j):
        mine = slice(256 * j, 256 * (j + 1))
        k, v = qkv[1, mine, :], qkv[2, mine, :]
        row = lax.broadcasted_iota(jnp.int32, (256, 1), 0) + 256 * j
        dk = jnp.zeros((256, 128), F32)
        dv = jnp.zeros((256, 128), F32)
        for lo in range(256 * j, 2048, 512):
            n = min(512, 2048 - lo)
            rows = slice(lo, lo + n)
            col = lax.broadcasted_iota(jnp.int32, (1, n), 1) + lo
            q, d = qkv[0, rows, :], do[rows, :]
            sig = jax.nn.sigmoid(dot_t(k, q) * SCALE + bias_at(col, lens))
            visible = row >= document_start(col, lens)
            if lo == 256 * j:
                visible = visible & (row <= col)
            sig = jnp.where(visible, sig, 0.0)
            dv = dv + dot(sig.astype(BF), d)
            ds = (dot_t(v, d) * sig * (1.0 - sig)).astype(BF)
            dk = dk + dot(ds, q)
            dq[rows, :] += t_dot(ds, k)
        put(j, unrotate(dk, j), 1)
        put(j, dv.astype(BF), 2)

    ring.far(0, ff, far)
    ring.far(1, ff, far)
    total[...] = jnp.zeros_like(total)
    dq[...] = jnp.zeros_like(dq)
    arrive()
    products(SCATTER_ORDER)
    ring.near(0, ff, far, near)
    arrive()
    ring.near(1, ff, far, near)
    arrive()
    arrive()
    arrive()
    arrive()
    next(back)
    arrive()
    ring.join(0, ff, near, chunk)
    ring.across(0, chunk, box)
    arrive()
    grad_out[...] = total[...].astype(BF)
    keys(0)
    next(back)
    ring.join(1, ff, near, chunk)
    ring.across(1, chunk, box)
    keys(1)
    keys(2)
    next(back)
    ring.crossed(0, chunk, box, whole)
    keys(3)
    keys(4)
    next(back)
    keys(5)
    keys(6)
    ring.crossed(1, chunk, box, whole)
    ring.share(0, whole)
    keys(7)
    for i in range(8):
        put(i, unrotate(dq[256 * i : 256 * (i + 1), :], i), 0)
    run(back)

    def last(cols):
        mixed[:, cols] = (residual[:, cols] + sums.total(cols)).astype(BF)

    columns(2048, last)
    ring.share(1, whole)
    ring.shared(0)
    ring.shared(1)
    net.finish()


def attention_back(*args):
    return call(
        attention_back_kernel,
        "attention_back",
        3,
        [
            ((2048, 384), BF),
            ((128, 2048), BF),
            ((128, 2048), BF),
            ((3 * FF_ROWS, 2048), BF),
        ],
        [pltpu.VMEM((16, 128, 2048), BF)]
        + scatter_scratch(2048)
        + ring_sum_scratch(3 * FF_ROWS)
        + [pltpu.VMEM((2, 3 * FF_ROWS, 256), BF), pltpu.VMEM((2, 3 * FF_ROWS, 256), BF)]
        + [
            pltpu.VMEM((128, 2048), F32),
            pltpu.VMEM((2048, 128), BF),
            pltpu.VMEM((2048, 128), F32),
        ]
        + sems(N_GATHER + N_SCATTER + N_RING_SUM + N_RING_SHARE),
        args,
    )


def local(
    acts,
    doc_lengths,
    w_query,
    w_key,
    w_value,
    w_out,
    w_gate,
    w_up,
    w_down,
    gain_attn,
    gain_mlp,
    cotangent,
):
    tok = acts.shape[2]
    width = acts.shape[3]
    head = w_query.shape[1]
    ff = w_gate.shape[1]

    acts_rows = acts.reshape(tok, width)
    cot_low = cotangent.reshape(tok, width)
    gains = jnp.zeros((16, head), BF).at[0].set(gain_attn).at[1].set(gain_mlp)
    lens = jnp.broadcast_to(
        jnp.concatenate([doc_lengths.reshape(2), jnp.zeros((6,), jnp.int32)])[:, None], (8, head)
    )
    lane = jnp.arange(head) % (head // 2)
    frequency = 10000.0 ** (-(lane.astype(F32) * 2.0 / head))
    frequency = jnp.broadcast_to(frequency, (8, head))
    normed, qkv, cosines, sines, gain_rows = project(
        acts_rows, gains, lens, frequency, w_query, w_key, w_value, 0
    )
    def padded(w):
        return jnp.pad(w, ((0, FF_PAD - ff), (0, 0)))

    ff_w = jnp.stack([padded(w_gate.T), padded(w_up.T), padded(w_down)])
    attended, residual, d_res, gain_two_part, hidden, ff_grads = middle(
        qkv, lens, w_out, cot_low, acts_rows, gain_rows[1:2], ff_w
    )
    d_qkv, grad_out, mixed, ff_sums = attention_back(
        d_res, attended, w_out, ff_grads, qkv, lens, cosines, sines, hidden, ff_w[2], residual
    )
    acts_grad, attn_sums, gain_grads = d_normed(
        d_qkv,
        jnp.concatenate([w_query.T, w_key.T, w_value.T]),
        normed,
        acts_rows,
        d_res,
        gain_rows[0:1],
        grad_out,
        gain_two_part,
        5,
    )

    def ff_grad(i):
        return ff_sums[i * FF_ROWS : i * FF_ROWS + ff].astype(F32)

    def attn_grad(i):
        return attn_sums[i * head : (i + 1) * head].astype(F32)

    return (
        mixed.reshape(1, 1, tok, width),
        acts_grad.reshape(1, 1, tok, width),
        attn_grad(0).T,
        attn_grad(1).T,
        attn_grad(2).T,
        attn_grad(3),
        ff_grad(0).T,
        ff_grad(1).T,
        ff_grad(2),
        gain_grads[1],
        gain_grads[0],
    )


def solution(mesh):
    row = P("grp", "ctx", None, None)
    col = P(None, "ctx")
    dep = P("ctx", None)
    vec = P("ctx")
    in_specs = (row, P("grp", None), col, col, col, dep, col, col, dep, vec, vec, row)
    out_specs = (row, row, col, col, col, dep, col, col, dep, vec, vec)
    return jax.shard_map(local, mesh=mesh, in_specs=in_specs, out_specs=out_specs, check_vma=False)
```

```python
import math

import jax
import jax.numpy as jnp
import numpy as np
from jax import lax
from jax.experimental import pallas as pl
from jax.experimental.pallas import tpu as pltpu
from jax.sharding import PartitionSpec as P

EPSILON = 1e-05
BF = jnp.bfloat16
F32 = jnp.float32
MESH = pl.DeviceIdType.MESH
VM = pl.BlockSpec(memory_space=pltpu.VMEM)
FF_ROWS = 352
FF_PAD = 384


def dot(a, b):
    return jnp.dot(a, b, preferred_element_type=F32)


def dot_t(a, b):
    return lax.dot_general(a, b, (((1,), (1,)), ((), ())), preferred_element_type=F32)


def t_dot(a, b):
    return lax.dot_general(a, b, (((0,), (0,)), ((), ())), preferred_element_type=F32)


def place():
    c, g = lax.axis_index("ctx"), lax.axis_index("grp")
    return c // 8, (c // 2) % 4, c % 2, g // 4, g % 4


def slot_at(pos, dz, dy, dk=0):
    z, y, k = pos[:3]
    return ((z + dz) % 2) * 8 + ((y + dy) % 4) * 2 + (k + dk) % 2


HOPS = {"p": (0, 1, 0), "m": (0, 3, 0), "z": (1, 0, 0), "c": (0, 0, 1)}
GROUP_HOPS = {"e": (0, 1), "w": (0, 3), "h": (1, 0)}


def neighbour(pos, link):
    if link in HOPS:
        return (lax.axis_index("grp"), slot_at(pos, *HOPS[link]))
    dh, dx = GROUP_HOPS[link]
    return (((pos[3] + dh) % 2) * 4 + (pos[4] + dx) % 4, lax.axis_index("ctx"))


def ctx_peer(d):
    return (lax.axis_index("grp"), (lax.axis_index("ctx") + d) % 16)


def grp_peer(d):
    return ((lax.axis_index("grp") + d) % 8, lax.axis_index("ctx"))


def greet(targets):
    barrier = pltpu.get_barrier_semaphore()
    for t in targets:
        pl.semaphore_signal(barrier, inc=1, device_id=t, device_id_type=MESH)
    pl.semaphore_wait(barrier, len(targets))


class Copies:
    def __init__(self, pos, send, recv):
        self.pos, self.send, self.recv, self.all = pos, send, recv, {}
        self.unsent, self.count = {}, 0

    def start(self, name, target, src, dst):
        n, self.count = self.count, self.count + 1
        if isinstance(target, str):
            target = neighbour(self.pos, target)
        copy = pltpu.make_async_remote_copy(
            src_ref=src,
            dst_ref=dst,
            send_sem=self.send.at[n],
            recv_sem=self.recv.at[n],
            device_id=target,
            device_id_type=MESH,
        )
        copy.start()
        self.all[name] = self.unsent[name] = copy

    def got(self, *names):
        for name in names:
            self.all[name].wait_recv()

    def sent(self, name):
        self.unsent.pop(name).wait_send()

    def finish(self):
        for name in list(self.unsent):
            self.sent(name)


def columns(width, body, step=512):
    def tile(j, _):
        body(pl.ds(pl.multiple_of(j * step, step), step))
        return 0

    lax.fori_loop(0, width // step, tile, 0)


def add_to(dst, *srcs):
    def tile(cols):
        total = dst[:, cols].astype(F32)
        for s in srcs:
            total = total + s[:, cols].astype(F32)
        dst[:, cols] = total.astype(dst.dtype)

    columns(dst.shape[1], tile)


N_GATHER = 37


def gather_steps(net, pos, buf, tag):
    def send(name, link, dz, dy, lo, n):
        ref = buf.at[slot_at(pos, dz, dy), pl.ds(lo, n)]
        net.start(tag + name, link, ref, ref)

    def got(*names):
        net.got(*[tag + name for name in names])

    send("p1a", "p", 0, 0, 0, 64)
    send("m1a", "m", 0, 0, 64, 64)
    send("z0", "z", 0, 0, 32, 64)
    send("c0", "c", 0, 0, 0, 128)
    send("p1b", "p", 0, 0, 64, 64)
    send("m1b", "m", 0, 0, 0, 64)
    send("zb00", "z", 0, 0, 0, 32)
    send("zb01", "z", 0, 0, 96, 32)
    got("c0")
    yield 0, 0
    got("p1a")
    send("p2", "p", 0, 3, 0, 64)
    send("zb30", "z", 0, 3, 0, 32)
    got("m1a")
    send("m2", "m", 0, 1, 64, 64)
    send("zb11", "z", 0, 1, 96, 32)
    got("z0")
    send("p3", "p", 1, 0, 32, 64)
    send("m3", "m", 1, 0, 32, 64)
    send("c3", "c", 1, 0, 32, 64)
    yield None
    got("p1b")
    send("zb31", "z", 0, 3, 96, 32)
    send("c1", "c", 0, 3, 0, 128)
    got("m1b")
    send("zb10", "z", 0, 1, 0, 32)
    send("c2", "c", 0, 1, 0, 128)
    got("zb00", "zb01")
    send("c4", "c", 1, 0, 0, 32)
    send("c5", "c", 1, 0, 96, 32)
    got("c1")
    yield 0, 3
    got("c2")
    yield 0, 1
    got("p2")
    send("zb20", "z", 0, 2, 0, 32)
    send("c6", "c", 0, 2, 0, 64)
    got("m2")
    send("zb21", "z", 0, 2, 96, 32)
    send("c7", "c", 0, 2, 64, 64)
    yield None
    got("c3", "c4", "c5")
    yield 1, 0
    got("p3")
    send("p4", "p", 1, 3, 32, 32)
    send("c8", "c", 1, 3, 32, 64)
    got("m3")
    send("m4", "m", 1, 1, 64, 32)
    send("c9", "c", 1, 1, 32, 64)
    yield None
    got("c6", "c7")
    yield 0, 2
    got("zb30", "zb31")
    send("c10", "c", 1, 3, 0, 32)
    send("c11", "c", 1, 3, 96, 32)
    got("zb10", "zb11")
    send("c12", "c", 1, 1, 0, 32)
    send("c13", "c", 1, 1, 96, 32)
    got("p4")
    send("c14", "c", 1, 2, 32, 32)
    got("m4")
    send("c15", "c", 1, 2, 64, 32)
    yield None
    got("zb20")
    send("c16", "c", 1, 2, 0, 32)
    got("zb21")
    send("c17", "c", 1, 2, 96, 32)
    got("c14", "c15", "c16", "c17")
    yield 1, 2
    got("c9", "c12", "c13")
    yield 1, 1
    got("c8", "c10", "c11")
    yield 1, 3


def gather_round_steps(net, pos, buf, tag):
    def send(name, link, dz, dy, lo=0, n=128):
        ref = buf.at[slot_at(pos, dz, dy), pl.ds(lo, n)]
        net.start(tag + name, link, ref, ref)

    def got(*names):
        net.got(*[tag + name for name in names])

    send("z0", "z", 0, 0)
    send("p1a", "p", 0, 0, 0, 64)
    send("m1a", "m", 0, 0, 64, 64)
    send("c0", "c", 0, 0)
    send("p1b", "p", 0, 0, 64, 64)
    send("m1b", "m", 0, 0, 0, 64)
    got("c0")
    yield 0, 0
    got("p1a")
    send("p2", "p", 0, 3, 0, 64)
    got("m1a")
    send("m2", "m", 0, 1, 64, 64)
    got("z0")
    send("p3a", "p", 1, 0, 0, 64)
    send("m3a", "m", 1, 0, 64, 64)
    send("p3b", "p", 1, 0, 64, 64)
    send("m3b", "m", 1, 0, 0, 64)
    send("c3", "c", 1, 0)
    got("p1b")
    send("c1", "c", 0, 3)
    got("m1b")
    send("c2", "c", 0, 1)
    got("c1")
    yield 0, 3
    got("c2")
    yield 0, 1
    got("p2")
    send("c4", "c", 0, 2, 0, 64)
    got("m2")
    send("c5", "c", 0, 2, 64, 64)
    got("c3")
    yield 1, 0
    got("p3a")
    send("p4", "p", 1, 3, 0, 64)
    got("m3a")
    send("m4", "m", 1, 1, 64, 64)
    got("c4", "c5")
    yield 0, 2
    got("p3b")
    send("c6", "c", 1, 3)
    got("m3b")
    send("c7", "c", 1, 1)
    got("c6")
    yield 1, 3
    got("c7")
    yield 1, 1
    got("p4")
    send("c8", "c", 1, 2, 0, 64)
    got("m4")
    send("c9", "c", 1, 2, 64, 64)
    got("c8", "c9")
    yield 1, 2


N_SCATTER = 29
INBOX_ROWS = 896


def scatter_scratch(w):
    return [
        pltpu.VMEM((16, 128, w), BF),
        pltpu.VMEM((8, 128, w), BF),
        pltpu.VMEM((INBOX_ROWS, w), BF),
    ]


class Scatter:
    def __init__(self, net, pos, part, sib, inbox, tag, z_last=False):
        self.net, self.pos, self.part, self.sib, self.tag = net, pos, part, sib, tag
        self.box, at = {}, 0
        if z_last:
            rows = [(side + step, n) for step, n in zip("4321", (64, 128, 64, 128)) for side in "pm"]
            rows.append(("z0", 128))
        else:
            rows = [("zb%d%d" % (dy, h), 32) for dy in range(4) for h in range(2)]
            rows += [(side + step, n) for step, n in zip("4321", (32, 64, 64, 128)) for side in "pm"]
            rows.append(("z0", 64))
        for key, n in rows:
            self.box[key] = inbox.at[pl.ds(at, n)]
            at += n
        for side in "pm":
            whole = self.box[side + "1"]
            self.box[side + "1a"] = whole.at[pl.ds(32, 64)]
            self.box[side + "1b"] = whole.at[pl.ds(0, 32)]
            self.box[side + "1c"] = whole.at[pl.ds(96, 32)]

    def mine(self, dz, dy, lo=0, n=128):
        return self.part.at[slot_at(self.pos, dz, dy), pl.ds(lo, n)]

    def swap(self, dz, dy):
        src = self.part.at[slot_at(self.pos, dz, dy, 1)]
        self.net.start(self.tag + "c%d%d" % (dz, dy), "c", src, self.sib.at[dz * 4 + dy])

    def joined(self, dz, dy):
        self.got("c%d%d" % (dz, dy))
        add_to(self.mine(dz, dy), self.sib.at[dz * 4 + dy])

    def got(self, *names):
        self.net.got(*[self.tag + name for name in names])

    def put(self, name, link, src):
        self.net.start(self.tag + name, link, src, self.box[name])

    def put_zb(self, dy):
        for h, lo in ((0, 0), (1, 96)):
            self.put("zb%d%d" % (dy, h), "z", self.mine(1, dy, lo, 32))

    def take(self, name, dz, dy, lo, n):
        self.got(name)
        add_to(self.mine(dz, dy, lo, n), self.box[name])

    def take_zb(self, dy):
        self.take("zb%d0" % dy, 0, dy, 0, 32)
        self.take("zb%d1" % dy, 0, dy, 96, 32)

    def steps(self):
        self.joined(1, 2)
        self.put_zb(2)
        self.put("p4", "p", self.mine(1, 2, 64, 32))
        self.put("m4", "m", self.mine(1, 2, 32, 32))
        yield
        self.joined(1, 1)
        self.put_zb(1)
        self.joined(1, 3)
        self.put_zb(3)
        yield
        self.take("p4", 1, 1, 64, 32)
        self.put("p3", "p", self.mine(1, 1, 32, 64))
        self.take("m4", 1, 3, 32, 32)
        self.put("m3", "m", self.mine(1, 3, 32, 64))
        yield
        self.joined(0, 2)
        self.take_zb(2)
        self.put("p2", "p", self.mine(0, 2, 64, 64))
        self.put("m2", "m", self.mine(0, 2, 0, 64))
        yield
        self.joined(1, 0)
        self.joined(0, 1)
        self.joined(0, 3)
        self.joined(0, 0)
        yield
        self.take("p3", 1, 0, 32, 64)
        self.take("m3", 1, 0, 32, 64)
        self.put("z0", "z", self.mine(1, 0, 32, 64))
        self.put_zb(0)
        yield
        self.take("p2", 0, 1, 64, 64)
        self.put("p1a", "p", self.mine(0, 1, 32, 64))
        self.take("m2", 0, 3, 0, 64)
        self.put("m1a", "m", self.mine(0, 3, 32, 64))
        yield
        self.take_zb(1)
        self.put("p1b", "p", self.mine(0, 1, 0, 32))
        self.put("p1c", "p", self.mine(0, 1, 96, 32))
        self.take_zb(3)
        self.put("m1b", "m", self.mine(0, 3, 0, 32))
        self.put("m1c", "m", self.mine(0, 3, 96, 32))
        yield
        self.take("z0", 0, 0, 32, 64)
        self.take_zb(0)
        yield
        self.got("p1a", "m1a", "p1b", "p1c", "m1b", "m1c")

    def z_last_steps(self):
        self.joined(1, 2)
        self.put("p4", "p", self.mine(1, 2, 64, 64))
        self.put("m4", "m", self.mine(1, 2, 0, 64))
        self.joined(0, 2)
        self.put("p2", "p", self.mine(0, 2, 64, 64))
        self.put("m2", "m", self.mine(0, 2, 0, 64))
        self.joined(1, 1)
        self.joined(1, 3)
        yield
        self.take("p4", 1, 1, 64, 64)
        self.put("p3", "p", self.mine(1, 1))
        self.take("m4", 1, 3, 0, 64)
        self.put("m3", "m", self.mine(1, 3))
        self.joined(0, 1)
        self.joined(0, 3)
        yield
        self.take("p2", 0, 1, 64, 64)
        self.put("p1", "p", self.mine(0, 1))
        self.take("m2", 0, 3, 0, 64)
        self.put("m1", "m", self.mine(0, 3))
        self.joined(1, 0)
        self.joined(0, 0)
        yield
        self.take("p3", 1, 0, 0, 128)
        self.take("m3", 1, 0, 0, 128)
        self.put("z0", "z", self.mine(1, 0))
        yield
        self.take("z0", 0, 0, 0, 128)
        self.got("p1", "m1")

    def total(self, cols):
        sums = self.mine(0, 0)[:, cols].astype(F32)
        return sums + self.box["p1"][:, cols].astype(F32) + self.box["m1"][:, cols].astype(F32)


SCATTER_ORDER = [(1, 2), (1, 1), (1, 3), (1, 0), (0, 2), (0, 1), (0, 3), (0, 0)]


def pair_rows(pos, dz, dy):
    first = slot_at(pos, dz, dy) // 2
    return first * 2, pl.ds(pl.multiple_of(first * 256, 256), 256)


def product(pos, part, dz, dy, *factors):
    slot, rows = pair_rows(pos, dz, dy)

    def tile(cols):
        total = None
        for a, b in factors:
            term = dot(a[rows, :], b[:, cols])
            total = term if total is None else total + term
        part[slot, :, cols] = total[:128].astype(BF)
        part[slot + 1, :, cols] = total[128:].astype(BF)

    columns(part.shape[2], tile)


def quarter(pos, d, half=None):
    start = ((pos[4] + d) % 4) * 256
    if half is None:
        return pl.ds(pl.multiple_of(start, 256), 256)
    return pl.ds(pl.multiple_of(start + half * 128, 128), 128)


def part_columns(pos, d, p):
    return pl.ds(pl.multiple_of(((pos[4] + d) % 4) * 512 + p * 256, 256), 256)


def by_rows(rows, body):
    def step(i, _):
        body(pl.ds(pl.multiple_of(i * 32, 32), 32))
        return 0

    lax.fori_loop(0, rows // 32, step, 0)


def ring_sum_scratch(rows):
    return [pltpu.VMEM((2, rows, 128), BF), pltpu.VMEM((2, rows, 256), BF)]


N_RING_SUM = 4
N_RING_SHARE = 5


class Ring:
    def __init__(self, net, pos, tag):
        self.net, self.pos, self.tag = net, pos, tag

    def put(self, name, link, src, dst):
        self.net.start(self.tag + name, link, src, dst)

    def got(self, *names):
        self.net.got(*[self.tag + name for name in names])

    def far(self, terms, far):
        self.put("e2", "e", terms.at[:, quarter(self.pos, 2, 0)], far.at[0])
        self.put("w2", "w", terms.at[:, quarter(self.pos, 2, 1)], far.at[1])

    def near(self, terms, far, near):
        for name, d, half in (("e", 1, 0), ("w", 3, 1)):
            self.got(name + "2")
            cols = quarter(self.pos, d, half)

            def fold(r, half=half, cols=cols):
                total = terms[r, cols].astype(F32) + far[half, r, :].astype(F32)
                terms[r, cols] = total.astype(BF)

            by_rows(terms.shape[0], fold)
            self.put(name + "1", name, terms.at[:, quarter(self.pos, d)], near.at[half])

    def join(self, terms, near, chunk):
        self.got("e1", "w1")

        def add(r):
            total = terms[r, quarter(self.pos, 0)].astype(F32) + near[0, r, :].astype(F32)
            chunk[r, :] = (total + near[1, r, :].astype(F32)).astype(BF)

        by_rows(terms.shape[0], add)

    def across(self, chunk, box):
        self.put("h", "h", chunk, box)

    def crossed(self, chunk, box, whole):
        self.got("h")
        cols = quarter(self.pos, 0)

        def add(r):
            whole[r, cols] = (chunk[r, :].astype(F32) + box[r, :].astype(F32)).astype(BF)

        by_rows(whole.shape[0], add)
        for name in "ew":
            self.put(name + "3", name, whole.at[:, cols], whole.at[:, cols])

    def share(self, whole):
        for name, d, half in (("e", 3, 0), ("w", 1, 1)):
            self.got(name + "3")
            ref = whole.at[:, quarter(self.pos, d, half)]
            self.put(name + "4", name, ref, ref)

    def shared(self):
        self.got("e4", "w4")


def run(*steps):
    steps = list(steps)
    while steps:
        for s in list(steps):
            try:
                next(s)
            except StopIteration:
                steps.remove(s)


def sems(n):
    return [pltpu.SemaphoreType.DMA((n,)), pltpu.SemaphoreType.DMA((n,))]


HBM = pl.BlockSpec(memory_space=pl.ANY)


def call(kernel, name, cid, outs, scratch, args, mib=60, in_hbm=(), out_hbm=()):
    return pl.pallas_call(
        kernel,
        out_shape=[jax.ShapeDtypeStruct(s, d) for s, d in outs],
        in_specs=[HBM if i in in_hbm else VM for i in range(len(args))],
        out_specs=[HBM if i in out_hbm else VM for i in range(len(outs))],
        scratch_shapes=scratch,
        compiler_params=pltpu.CompilerParams(
            collective_id=cid, has_side_effects=True, vmem_limit_bytes=mib * 2**20
        ),
        name=name,
    )(*args)


def norm_factor(u):
    return lax.rsqrt(jnp.mean(u * u, -1, keepdims=True) + EPSILON)


def d_normed_kernel(
    d_qkv,
    w,
    far_normed,
    acts,
    d_res,
    gain,
    grad_out,
    gain_two_part,
    acts_grad,
    whole,
    gains,
    normed,
    part,
    sib,
    inbox,
    terms,
    chunk,
    box,
    far0,
    near0,
    far1,
    near1,
    low_t,
    gain_terms,
    gain_box,
    gain_sum,
    gain_wide,
    send,
    recv,
    in_sem,
):
    pos = place()
    net = Copies(pos, send, recv)
    me = lax.axis_index("ctx")
    fetch = pltpu.make_async_copy(far_normed, normed, in_sem)
    fetch.start()
    greet([ctx_peer(d) for d in range(1, 16)] + [grp_peer(d) for d in range(1, 8)])
    sums = Scatter(net, pos, part, sib, inbox, "s", True)
    low_t[...] = d_qkv[...].T
    for q in range(4):
        for p in range(2):
            cols = slice(q * 512 + p * 256, q * 512 + p * 256 + 256)
            terms[p, pl.ds(384, 128), q * 256 : (q + 1) * 256] = grad_out[:, cols]
    gain_terms[...] = jnp.zeros_like(gain_terms)
    for j in range(16):
        cols = slice(j * 128, (j + 1) * 128)
        gain_terms[j, 0:1, :] = gain_two_part[:, cols]

    def weight_grads(d, p):
        cols = part_columns(pos, d, p)
        g = dot(low_t[...], normed[:, :, cols].reshape(2048, 256))
        terms[p, pl.ds(0, 384), quarter(pos, d)] = g.astype(BF)
        by_column = jnp.sum(g * w[:, cols].astype(F32), 0, keepdims=True) / gain[:, cols]
        first = ((pos[4] + d) % 4) * 4 + p * 2
        gain_terms[first, 1:2, :] = by_column[:, :128]
        gain_terms[first + 1, 1:2, :] = by_column[:, 128:]

    def products(pairs):
        for dz, dy in pairs:
            product(pos, part, dz, dy, (d_qkv, w))
            sums.swap(dz, dy)

    back = sums.z_last_steps()
    rings = Ring(net, pos, "r"), Ring(net, pos, "q")
    boxes = (far0, near0), (far1, near1)
    products(SCATTER_ORDER[:2])
    fetch.wait()
    weight_grads(2, 0)
    rings[0].far(terms.at[0], far0)
    products(SCATTER_ORDER[2:4])
    weight_grads(2, 1)
    rings[1].far(terms.at[1], far1)
    products(SCATTER_ORDER[4:])
    next(back)
    weight_grads(1, 0)
    weight_grads(3, 0)
    rings[0].near(terms.at[0], far0, near0)
    next(back)
    weight_grads(1, 1)
    weight_grads(3, 1)
    rings[1].near(terms.at[1], far1, near1)
    next(back)
    weight_grads(0, 0)
    weight_grads(0, 1)
    for d in range(1, 16):
        net.start("g%d" % d, ctx_peer(d), gain_terms.at[(me + d) % 16], gain_box.at[d])
    gain_box[0] = gain_terms[me]
    for p in range(2):
        rings[p].join(terms.at[p], boxes[p][1], chunk.at[p])
        rings[p].across(chunk.at[p], box.at[p])
    next(back)
    rings[0].crossed(chunk.at[0], box.at[0], whole.at[0])
    net.got(*["g%d" % d for d in range(1, 16)])
    gain_sum[...] = jnp.sum(gain_box[...], 0)
    for d in range(1, 8):
        net.start("h%d" % d, grp_peer(d), gain_sum, gain_wide.at[d])
    gain_wide[0] = gain_sum[...]
    rings[1].crossed(chunk.at[1], box.at[1], whole.at[1])
    rings[0].share(whole.at[0])
    run(back)
    rings[1].share(whole.at[1])
    net.got(*["h%d" % d for d in range(1, 8)])
    gains[...] = jnp.sum(gain_wide[...], 0)

    def finish(i, _):
        r = pl.ds(pl.multiple_of(i * 32, 32), 32)
        e = (
            part[me, r, :].astype(F32)
            + sums.box["p1"][r, :].astype(F32)
            + sums.box["m1"][r, :].astype(F32)
        )
        u = acts[r, :].astype(F32)
        f = norm_factor(u)
        scaled = e * gain[...]
        grad = f * scaled - u * f * f * f * jnp.mean(scaled * u, -1, keepdims=True)
        acts_grad[r, :] = d_res[r, :] + grad
        return 0

    lax.fori_loop(0, 4, finish, 0)
    rings[0].shared()
    rings[1].shared()
    net.finish()


def d_normed(*args):
    return call(
        d_normed_kernel,
        "d_normed",
        3,
        [((128, 2048), F32), ((2, 512, 1024), BF), ((8, 128), F32)],
        [pltpu.VMEM((16, 128, 2048), BF)]
        + scatter_scratch(2048)
        + [pltpu.VMEM((2, 512, 1024), BF)]
        + [pltpu.VMEM((2, 512, 256), BF), pltpu.VMEM((2, 512, 256), BF)]
        + ring_sum_scratch(512)
        + ring_sum_scratch(512)
        + [
            pltpu.VMEM((384, 2048), BF),
            pltpu.VMEM((16, 8, 128), F32),
            pltpu.VMEM((16, 8, 128), F32),
            pltpu.VMEM((8, 128), F32),
            pltpu.VMEM((8, 8, 128), F32),
        ]
        + sems(N_SCATTER + 2 * N_RING_SUM + 2 * N_RING_SHARE + 22)
        + [pltpu.SemaphoreType.DMA],
        args,
        in_hbm=(2,),
    )


def widen_kernel(ff, attn, gate, up, down, query, key, value, out):
    for i, ref in enumerate((gate, up, down)):
        ref[...] = ff[0, i * FF_ROWS : i * FF_ROWS + ref.shape[0], :].astype(F32)
    for i, ref in enumerate((query, key, value)):
        ref[...] = attn[0, i * 128 : (i + 1) * 128, :].astype(F32).T
    out[...] = attn[0, 384:512, :].astype(F32)


def widen(ff_sums, attn_sums, ff):
    by_part = lambda j: (j % 2, 0, j // 2)
    column, row = lambda j: (0, j), lambda j: (j, 0)
    return pl.pallas_call(
        widen_kernel,
        grid=(8,),
        out_shape=[jax.ShapeDtypeStruct((ff, 2048), F32)] * 3
        + [jax.ShapeDtypeStruct((2048, 128), F32)] * 3
        + [jax.ShapeDtypeStruct((128, 2048), F32)],
        in_specs=[
            pl.BlockSpec((1, 3 * FF_ROWS, 256), by_part),
            pl.BlockSpec((1, 512, 256), by_part),
        ],
        out_specs=[pl.BlockSpec((ff, 256), column)] * 3
        + [pl.BlockSpec((256, 128), row)] * 3
        + [pl.BlockSpec((128, 256), column)],
        compiler_params=pltpu.CompilerParams(vmem_limit_bytes=40 * 2**20),
        name="widen",
    )(ff_sums, attn_sums)


def rope(u, cosine, sine):
    return u * cosine + pltpu.roll(u, 64, 1) * sine


def block_start(c, half):
    return c * 64 if half == 0 else (31 - c) * 64


def document_start(position, lens):
    first = lens[0:1, 0:1]
    return jnp.where(position >= first, first, 0)


def bias_at(position, lens):
    own = jnp.where(position >= lens[0:1, 0:1], lens[0:1, 1:2], lens[0:1, 0:1])
    return -jnp.log(own.astype(F32))


def project_kernel(
    x,
    gain_attn,
    gain_mlp,
    lens,
    frequency,
    w_query,
    w_key,
    w_value,
    w_gate_t,
    w_up_t,
    w_down,
    normed,
    qkv,
    cosines,
    sines,
    gain_rows,
    w_t,
    ff_in,
    ff_out,
    buf,
    normal,
    gain_box,
    w,
    send,
    recv,
    out_sem,
):
    pos = place()
    net = Copies(pos, send, recv)
    me = lax.axis_index("ctx")
    buf[me] = x[...]
    gain_box[me] = jnp.zeros((8, 128), F32)
    gain_box[me, 0:1, :] = gain_attn[...].astype(F32)
    gain_box[me, 1:2, :] = gain_mlp[...].astype(F32)
    greet([ctx_peer(d) for d in range(1, 16)])
    for d in range(1, 16):
        ref = gain_box.at[me]
        net.start("g%d" % d, ctx_peer(d), ref, ref)
    arrivals = gather_steps(net, pos, buf, "x")
    dz, dy = next(arrivals)

    def table(i, _):
        r = pl.ds(pl.multiple_of(i * 256, 256), 256)
        position = lax.broadcasted_iota(jnp.int32, (256, 128), 0) + i * 256
        offset = position - document_start(position, lens)
        angle = offset.astype(F32) * frequency[0:1, :]
        lane = lax.broadcasted_iota(jnp.int32, (256, 128), 1)
        cosines[r, :] = jnp.cos(angle)
        sines[r, :] = jnp.where(lane < 64, -1.0, 1.0) * jnp.sin(angle)
        return 0

    lax.fori_loop(0, 8, table, 0)
    for i, ref in enumerate((w_query, w_key, w_value)):
        w[:, i * 128 : (i + 1) * 128] = ref[...]
    net.got(*["g%d" % d for d in range(1, 16)])
    gain_rows[...] = jnp.zeros_like(gain_rows)
    for j in range(16):
        gain_rows[:, j * 128 : (j + 1) * 128] = gain_box[j]

    leaving = []
    done = 0
    while True:
        slot, _ = pair_rows(pos, dz, dy)

        def normalise(i, _, slot=slot):
            r = pl.ds(pl.multiple_of((i % 2) * 64, 64), 64)
            u = buf[slot + i // 2, r, :].astype(F32)
            normal[slot + i // 2, r, :] = (u * norm_factor(u) * gain_rows[0:1, :]).astype(BF)
            return 0

        lax.fori_loop(0, 4, normalise, 0)
        copy = pltpu.make_async_copy(
            normal.at[pl.ds(slot, 2)], normed.at[pl.ds(slot, 2)], out_sem.at[done]
        )
        copy.start()
        leaving.append(copy)
        out = dot(normal[pl.ds(slot, 2)].reshape(256, 2048), w[...])
        for b in range(2):
            for half in range(2):
                at = pl.ds(pl.multiple_of(block_start(slot + b, half), 64), 64)
                rows = slice(b * 128 + half * 64, b * 128 + half * 64 + 64)
                c, s = cosines[at, :], sines[at, :]
                qkv[0, at, :] = rope(out[rows, :128], c, s).astype(BF)
                qkv[1, at, :] = rope(out[rows, 128:256], c, s).astype(BF)
                qkv[2, at, :] = out[rows, 256:].astype(BF)
        done += 1
        if done == 1:
            w_t[...] = w[...].T
            for i, ref in enumerate((w_gate_t, w_up_t)):
                pad_rows(ff_in.at[i], ref)
            pad_rows(ff_out, w_down)
        if done == 8:
            break
        arrived = next(arrivals)
        while arrived is None:
            arrived = next(arrivals)
        dz, dy = arrived
    for _ in arrivals:
        pass
    for copy in leaving:
        copy.wait()
    net.finish()


def pad_rows(dst, src):
    rows = src.shape[0]
    dst[pl.ds(0, rows), :] = src[...]
    dst[pl.ds(rows, FF_PAD - rows), :] = jnp.zeros((FF_PAD - rows, dst.shape[1]), BF)


def project(*args):
    return call(
        project_kernel,
        "project",
        0,
        [
            ((16, 128, 2048), BF),
            ((3, 2048, 128), BF),
            ((2048, 128), F32),
            ((2048, 128), F32),
            ((8, 2048), F32),
            ((384, 2048), BF),
            ((2, FF_PAD, 2048), BF),
            ((FF_PAD, 2048), BF),
        ],
        [
            pltpu.VMEM((16, 128, 2048), BF),
            pltpu.VMEM((16, 128, 2048), BF),
            pltpu.VMEM((16, 8, 128), F32),
            pltpu.VMEM((2048, 384), BF),
        ]
        + sems(N_GATHER + 15)
        + [pltpu.SemaphoreType.DMA((8,))],
        args,
        out_hbm=(0,),
    )


SCALE = 1.0 / math.sqrt(128)


def attend_block(qkv, lens, i):
    q = qkv[0, 256 * i : 256 * (i + 1), :]
    row = lax.broadcasted_iota(jnp.int32, (256, 1), 0) + 256 * i
    start = document_start(row, lens)
    bias = bias_at(row, lens)
    total = jnp.zeros((256, 128), F32)
    for lo in range(0, 256 * (i + 1), 512):
        n = min(512, 256 * (i + 1) - lo)
        score = dot_t(q, qkv[1, lo : lo + n, :]) * SCALE + bias
        col = lax.broadcasted_iota(jnp.int32, (1, n), 1) + lo
        visible = col >= start
        if lo + n > 256 * i:
            visible = visible & (col <= row)
        prob = jnp.where(visible, jax.nn.sigmoid(score), 0.0).astype(BF)
        total = total + dot(prob, qkv[2, lo : lo + n, :])
    return total


def packed_start(block):
    return block * 128 if block < 16 else (31 - block) * 128 + 64


def middle_kernel(
    qkv,
    lens,
    w_out,
    cot,
    acts,
    gain,
    ff_in,
    ff_out,
    attended,
    residual,
    d_res,
    gain_part,
    hidden,
    chunk,
    later,
    cot_all,
    buf,
    low_t,
    part,
    sib,
    inbox,
    terms,
    far,
    near,
    send,
    recv,
):
    pos = place()
    net = Copies(pos, send, recv)
    me = lax.axis_index("ctx")
    cot_all[me] = cot[...]
    greet([neighbour(pos, l) for l in "pmzcew"])
    cots = gather_steps(net, pos, cot_all, "c")
    next(cots)
    for i in range(8):
        out = attend_block(qkv, lens, i).astype(BF)
        for b in range(4):
            at = packed_start(4 * i + b)
            attended[at : at + 64, :] = out[64 * b : 64 * (b + 1)]
        if i in (6, 7):
            next(cots)
    sums = Scatter(net, pos, part, sib, inbox, "a")
    for dz, dy in SCATTER_ORDER:
        product(pos, part, dz, dy, (attended, w_out))
        sums.swap(dz, dy)
    run(sums.steps(), cots)

    def normalise(i, _):
        r = pl.ds(pl.multiple_of(i * 32, 32), 32)
        u = (
            acts[r, :].astype(F32)
            + part[me, r, :].astype(F32)
            + sums.box["p1"][r, :].astype(F32)
            + sums.box["m1"][r, :].astype(F32)
        )
        residual[r, :] = u
        buf[me, r, :] = (u * norm_factor(u) * gain[...]).astype(BF)
        return 0

    lax.fori_loop(0, 4, normalise, 0)
    net.finish()
    sums = Scatter(net, pos, part, sib, inbox, "s")
    back = sums.steps()
    for arrived in gather_steps(net, pos, buf, "x"):
        if arrived is None:
            continue
        dz, dy = arrived
        slot, rows = pair_rows(pos, dz, dy)
        n2 = buf[pl.ds(slot, 2)].reshape(256, 2048)
        ct = cot_all[pl.ds(slot, 2)].reshape(256, 2048)
        gate = dot_t(n2, ff_in[0])
        up = dot_t(n2, ff_in[1])
        d_hidden = dot_t(ct, ff_out[...])
        sig = jax.nn.sigmoid(gate)
        silu = gate * sig
        h = (silu * up).astype(BF)
        dg = (d_hidden * up * sig * (1.0 + gate * (1.0 - sig))).astype(BF)
        du = (d_hidden * silu).astype(BF)
        hidden[rows, :] = h
        low_t[0, :, rows] = dg.T
        low_t[1, :, rows] = du.T
        low_t[2, :, rows] = h.T

        def tile(cols):
            t = dot(dg, ff_in[0, :, cols]) + dot(du, ff_in[1, :, cols])
            part[slot, :, cols] = t[:128].astype(BF)
            part[slot + 1, :, cols] = t[128:].astype(BF)

        columns(2048, tile)
        sums.swap(dz, dy)

        if (dz, dy) == (1, 1):
            next(back)

    def weight_grads(d, p, dst):
        cols, to = part_columns(pos, d, p), quarter(pos, d)
        for i, other in ((0, buf), (1, buf), (2, cot_all)):
            g = dot(low_t[i], other[:, :, cols].reshape(2048, 256))
            dst[pl.ds(i * FF_ROWS, FF_ROWS), to] = g[:FF_ROWS].astype(BF)

    ring = Ring(net, pos, "r")
    next(back)
    next(back)
    weight_grads(2, 0, terms)
    ring.far(terms, far)
    next(back)
    weight_grads(1, 0, terms)
    weight_grads(3, 0, terms)
    next(back)
    ring.near(terms, far, near)
    next(back)
    weight_grads(0, 0, terms)
    weight_grads(0, 1, later)
    next(back)
    weight_grads(1, 1, later)
    weight_grads(2, 1, later)
    next(back)
    weight_grads(3, 1, later)
    run(back)
    ring.join(terms, near, chunk)

    gain_part[...] = jnp.zeros_like(gain_part)

    def back(i, _):
        r = pl.ds(pl.multiple_of(i * 32, 32), 32)
        slot = me
        e = (
            part[slot, r, :].astype(F32)
            + sums.box["p1"][r, :].astype(F32)
            + sums.box["m1"][r, :].astype(F32)
        )
        u = residual[r, :]
        f = norm_factor(u)
        scaled = e * gain[...]
        grad = f * scaled - u * f * f * f * jnp.mean(scaled * u, -1, keepdims=True)
        d_res[r, :] = cot[r, :].astype(F32) + grad
        gain_part[...] += jnp.sum(e * u * f, 0, keepdims=True)
        return 0

    lax.fori_loop(0, 4, back, 0)
    net.finish()


def middle(*args):
    return call(
        middle_kernel,
        "middle",
        1,
        [
            ((2048, 128), BF),
            ((128, 2048), F32),
            ((128, 2048), F32),
            ((1, 2048), F32),
            ((2048, FF_PAD), BF),
            ((3 * FF_ROWS, 256), BF),
            ((3 * FF_ROWS, 1024), BF),
        ],
        [pltpu.VMEM((16, 128, 2048), BF), pltpu.VMEM((16, 128, 2048), BF)]
        + [pltpu.VMEM((3, FF_PAD, 2048), BF)]
        + scatter_scratch(2048)
        + [pltpu.VMEM((3 * FF_ROWS, 1024), BF)]
        + ring_sum_scratch(3 * FF_ROWS)
        + sems(2 * N_SCATTER + 2 * N_GATHER + N_RING_SUM),
        args,
        62,
    )


def attention_back_kernel(
    d_res,
    attended,
    w_out,
    chunk0,
    terms,
    qkv,
    lens,
    cosines,
    sines,
    hidden,
    w_down,
    residual,
    d_qkv,
    grad_out,
    mixed,
    whole,
    buf,
    part,
    sib,
    inbox,
    far,
    near,
    chunk1,
    box,
    total,
    do,
    dq,
    send,
    recv,
):
    pos = place()
    net = Copies(pos, send, recv)
    buf[lax.axis_index("ctx")] = d_res[...].astype(BF)
    greet([neighbour(pos, l) for l in "pmzcewh"])
    sums = Scatter(net, pos, part, sib, inbox, "s", True)
    back = sums.z_last_steps()
    rings = Ring(net, pos, "r"), Ring(net, pos, "q")
    arrivals = gather_round_steps(net, pos, buf, "x")

    def arrive():
        slot, rows = pair_rows(pos, *next(arrivals))
        d = buf[pl.ds(slot, 2)].reshape(256, 2048)
        g = dot_t(d, w_out[...]).astype(BF)
        for b in range(2):
            for half in range(2):
                at = pl.ds(pl.multiple_of(block_start(slot + b, half), 64), 64)
                do[at, :] = g[b * 128 + half * 64 : b * 128 + half * 64 + 64]
        total[...] += t_dot(attended[rows, :], d)

    def products(pairs):
        for dz, dy in pairs:
            product(pos, part, dz, dy, (hidden, w_down))
            sums.swap(dz, dy)

    def put(block, value, i):
        for b in range(4):
            at = packed_start(4 * block + b)
            d_qkv[at : at + 64, 128 * i : 128 * (i + 1)] = value[64 * b : 64 * (b + 1)]

    def unrotate(u, block):
        r = slice(256 * block, 256 * (block + 1))
        return rope(u * SCALE, cosines[r, :], -sines[r, :]).astype(BF)

    def keys(j):
        mine = slice(256 * j, 256 * (j + 1))
        k, v = qkv[1, mine, :], qkv[2, mine, :]
        row = lax.broadcasted_iota(jnp.int32, (256, 1), 0) + 256 * j
        dk = jnp.zeros((256, 128), F32)
        dv = jnp.zeros((256, 128), F32)
        for lo in range(256 * j, 2048, 512):
            n = min(512, 2048 - lo)
            rows = slice(lo, lo + n)
            col = lax.broadcasted_iota(jnp.int32, (1, n), 1) + lo
            q, d = qkv[0, rows, :], do[rows, :]
            sig = jax.nn.sigmoid(dot_t(k, q) * SCALE + bias_at(col, lens))
            visible = row >= document_start(col, lens)
            if lo == 256 * j:
                visible = visible & (row <= col)
            sig = jnp.where(visible, sig, 0.0)
            dv = dv + dot(sig.astype(BF), d)
            ds = (dot_t(v, d) * sig * (1.0 - sig)).astype(BF)
            dk = dk + dot(ds, q)
            dq[rows, :] += t_dot(ds, k)
        put(j, unrotate(dk, j), 1)
        put(j, dv.astype(BF), 2)

    rings[1].far(terms, far)
    total[...] = jnp.zeros_like(total)
    dq[...] = jnp.zeros_like(dq)
    arrive()
    rings[0].across(chunk0, box.at[0])
    products(SCATTER_ORDER)
    rings[1].near(terms, far, near)
    arrive()
    arrive()
    arrive()
    arrive()
    next(back)
    rings[0].crossed(chunk0, box.at[0], whole.at[0])
    arrive()
    rings[1].join(terms, near, chunk1)
    rings[1].across(chunk1, box.at[1])
    arrive()
    arrive()
    grad_out[...] = total[...].astype(BF)
    keys(0)
    next(back)
    rings[0].share(whole.at[0])
    keys(1)
    keys(2)
    next(back)
    rings[1].crossed(chunk1, box.at[1], whole.at[1])
    keys(3)
    keys(4)
    keys(5)
    next(back)
    keys(6)
    keys(7)
    rings[1].share(whole.at[1])
    for i in range(8):
        put(i, unrotate(dq[256 * i : 256 * (i + 1), :], i), 0)
    run(back)

    def last(cols):
        mixed[:, cols] = (residual[:, cols] + sums.total(cols)).astype(BF)

    columns(2048, last)
    rings[0].shared()
    rings[1].shared()
    net.finish()


def attention_back(*args):
    return call(
        attention_back_kernel,
        "attention_back",
        2,
        [
            ((2048, 384), BF),
            ((128, 2048), BF),
            ((128, 2048), BF),
            ((2, 3 * FF_ROWS, 1024), BF),
        ],
        [pltpu.VMEM((16, 128, 2048), BF)]
        + scatter_scratch(2048)
        + ring_sum_scratch(3 * FF_ROWS)
        + [pltpu.VMEM((3 * FF_ROWS, 256), BF), pltpu.VMEM((2, 3 * FF_ROWS, 256), BF)]
        + [
            pltpu.VMEM((128, 2048), F32),
            pltpu.VMEM((2048, 128), BF),
            pltpu.VMEM((2048, 128), F32),
        ]
        + sems(N_GATHER + N_SCATTER + N_RING_SUM + 2 * N_RING_SHARE),
        args,
    )


def local(
    acts,
    doc_lengths,
    w_query,
    w_key,
    w_value,
    w_out,
    w_gate,
    w_up,
    w_down,
    gain_attn,
    gain_mlp,
    cotangent,
):
    tok = acts.shape[2]
    width = acts.shape[3]
    head = w_query.shape[1]
    ff = w_gate.shape[1]

    acts_rows = acts.reshape(tok, width)
    cot_low = cotangent.reshape(tok, width)
    lane = np.arange(head) % (head // 2)
    frequency = 10000.0 ** (-(lane.astype(np.float64) * 2.0 / head))
    frequency = jnp.asarray(np.broadcast_to(frequency.astype(np.float32), (8, head)))
    normed, qkv, cosines, sines, gain_rows, w_t, ff_in, ff_out = project(
        acts_rows,
        gain_attn.reshape(1, head),
        gain_mlp.reshape(1, head),
        doc_lengths,
        frequency,
        w_query,
        w_key,
        w_value,
        w_gate.T,
        w_up.T,
        w_down,
    )
    attended, residual, d_res, gain_two_part, hidden, chunk, later = middle(
        qkv, doc_lengths, w_out, cot_low, acts_rows, gain_rows[1:2], ff_in, ff_out
    )
    d_qkv, grad_out, mixed, ff_sums = attention_back(
        d_res,
        attended,
        w_out,
        chunk,
        later,
        qkv,
        doc_lengths,
        cosines,
        sines,
        hidden,
        ff_out,
        residual,
    )
    acts_grad, attn_sums, gain_grads = d_normed(
        d_qkv, w_t, normed, acts_rows, d_res, gain_rows[0:1], grad_out, gain_two_part
    )
    gate, up, down, query, key, value, out = widen(ff_sums, attn_sums, ff)
    return (
        mixed.reshape(1, 1, tok, width),
        acts_grad.reshape(1, 1, tok, width),
        query,
        key,
        value,
        out,
        gate.T,
        up.T,
        down,
        gain_grads[1],
        gain_grads[0],
    )


def solution(mesh):
    row = P("grp", "ctx", None, None)
    col = P(None, "ctx")
    dep = P("ctx", None)
    vec = P("ctx")
    in_specs = (row, P("grp", None), col, col, col, dep, col, col, dep, vec, vec, row)
    out_specs = (row, row, col, col, col, dep, col, col, dep, vec, vec)
    return jax.shard_map(local, mesh=mesh, in_specs=in_specs, out_specs=out_specs, check_vma=False)
```

```python
import functools
import math

import jax
import jax.numpy as jnp
from jax import lax
from jax.experimental import pallas as pl
from jax.experimental.pallas import tpu as pltpu
from jax.sharding import PartitionSpec as P

EPSILON = 1e-05
CTX, GRP = "ctx", "grp"
BF = jnp.bfloat16
F32 = jnp.float32
MESH = pl.DeviceIdType.MESH
VM = pl.BlockSpec(memory_space=pltpu.VMEM)
FF_ROWS = 352
FF_PAD = 384


def dot(a, b):
    return jnp.dot(a, b, preferred_element_type=F32)


def dot_t(a, b):
    return lax.dot_general(a, b, (((1,), (1,)), ((), ())), preferred_element_type=F32)


def t_dot(a, b):
    return lax.dot_general(a, b, (((0,), (0,)), ((), ())), preferred_element_type=F32)


def place():
    c, g = lax.axis_index(CTX), lax.axis_index(GRP)
    return c // 8, (c // 2) % 4, c % 2, g // 4, g % 4


def slot_at(pos, dz, dy, dk=0):
    z, y, k = pos[:3]
    return ((z + dz) % 2) * 8 + ((y + dy) % 4) * 2 + (k + dk) % 2


HOPS = {"p": (0, 1, 0), "m": (0, 3, 0), "z": (1, 0, 0), "c": (0, 0, 1)}
GROUP_HOPS = {"e": (0, 1), "w": (0, 3), "h": (1, 0)}


def neighbour(pos, link):
    if link in HOPS:
        return (lax.axis_index(GRP), slot_at(pos, *HOPS[link]))
    dh, dx = GROUP_HOPS[link]
    return (((pos[3] + dh) % 2) * 4 + (pos[4] + dx) % 4, lax.axis_index(CTX))


def ctx_peer(d):
    return (lax.axis_index(GRP), (lax.axis_index(CTX) + d) % 16)


def grp_peer(d):
    return ((lax.axis_index(GRP) + d) % 8, lax.axis_index(CTX))


def greet(targets):
    barrier = pltpu.get_barrier_semaphore()
    for t in targets:
        pl.semaphore_signal(barrier, inc=1, device_id=t, device_id_type=MESH)
    pl.semaphore_wait(barrier, len(targets))


class Copies:
    def __init__(self, pos, send, recv):
        self.pos, self.send, self.recv, self.all = pos, send, recv, {}
        self.unsent, self.count = {}, 0

    def start(self, name, target, src, dst):
        n, self.count = self.count, self.count + 1
        if isinstance(target, str):
            target = neighbour(self.pos, target)
        copy = pltpu.make_async_remote_copy(
            src_ref=src,
            dst_ref=dst,
            send_sem=self.send.at[n],
            recv_sem=self.recv.at[n],
            device_id=target,
            device_id_type=MESH,
        )
        copy.start()
        self.all[name] = self.unsent[name] = copy

    def got(self, *names):
        for name in names:
            self.all[name].wait_recv()

    def sent(self, name):
        self.unsent.pop(name).wait_send()

    def finish(self):
        for name in list(self.unsent):
            self.sent(name)


def columns(width, body, step=512):
    for at in range(0, width, step):
        body(slice(at, at + step))


def apart(body):
    pl.when(lax.axis_index(CTX) >= 0)(body)


def add_to(dst, src):
    def tile(cols):
        dst[:, cols] = dst[:, cols] + src[:, cols]

    apart(lambda: columns(dst.shape[1], tile))


def perform(actions, order):
    names = sorted(actions)
    assert sorted(order) == list(range(len(names)))
    for i in order:
        actions[names[i]]()


N_GATHER = 37


def gather_actions(net, pos, buf, tag, top):
    z_first = top == 0
    lo, n = (0, 128) if z_first else (32, top - 32)
    rest = 128 - top

    def send(name, link, dz, dy, lo=0, n=128):
        ref = buf.at[slot_at(pos, dz, dy), pl.ds(lo, n)]
        net.start(tag + name, link, ref, ref)

    table = {
        "first": [
            [],
            [
                ("z0", "z", 0, 0, lo, n),
                ("p1a", "p", 0, 0, 0, 64),
                ("m1a", "m", 0, 0, 64, 64),
                ("c0", "c", 0, 0),
                ("p1b", "p", 0, 0, 64, 64),
                ("m1b", "m", 0, 0, 0, 64),
            ],
        ],
        "in00": [["c0"], []],
        "in03": [["c1"], []],
        "in01": [["c2"], []],
        "in02": [["c6", "c7"], []],
    }
    if z_first:
        table["p1a"] = [["p1a"], [("p2", "p", 0, 3, 0, 64)]]
        table["m1a"] = [["m1a"], [("m2", "m", 0, 1, 64, 64)]]
        table["z0"] = [
            ["z0"],
            [
                ("p3a", "p", 1, 0, 0, 64),
                ("m3a", "m", 1, 0, 64, 64),
                ("p3b", "p", 1, 0, 64, 64),
                ("m3b", "m", 1, 0, 0, 64),
                ("c3", "c", 1, 0),
            ],
        ]
        table["p1b"] = [["p1b"], [("c1", "c", 0, 3)]]
        table["m1b"] = [["m1b"], [("c2", "c", 0, 1)]]
        table["p2"] = [["p2"], [("c6", "c", 0, 2, 0, 64)]]
        table["m2"] = [["m2"], [("c7", "c", 0, 2, 64, 64)]]
        table["p3a"] = [["p3a"], [("p4", "p", 1, 3, 0, 64)]]
        table["m3a"] = [["m3a"], [("m4", "m", 1, 1, 64, 64)]]
        table["p3b"] = [["p3b"], [("c8", "c", 1, 3)]]
        table["m3b"] = [["m3b"], [("c9", "c", 1, 1)]]
        table["p4"] = [["p4"], [("c14", "c", 1, 2, 0, 64)]]
        table["m4"] = [["m4"], [("c15", "c", 1, 2, 64, 64)]]
        table["in10"] = [["c3"], []]
        table["in13"] = [["c8"], []]
        table["in11"] = [["c9"], []]
        table["in12"] = [["c14", "c15"], []]
    else:
        table["first"][1] += [("zb00", "z", 0, 0, 0, 32), ("zb01", "z", 0, 0, top, rest)]
        table["p1a"] = [["p1a"], [("p2", "p", 0, 3, 0, 64), ("zb30", "z", 0, 3, 0, 32)]]
        table["m1a"] = [["m1a"], [("m2", "m", 0, 1, 64, 64), ("zb11", "z", 0, 1, top, rest)]]
        table["z0"] = [
            ["z0"],
            [("p3", "p", 1, 0, lo, n), ("m3", "m", 1, 0, lo, n), ("c3", "c", 1, 0, lo, n)],
        ]
        table["p1b"] = [["p1b"], [("zb31", "z", 0, 3, top, rest), ("c1", "c", 0, 3)]]
        table["m1b"] = [["m1b"], [("zb10", "z", 0, 1, 0, 32), ("c2", "c", 0, 1)]]
        table["zb0"] = [["zb00", "zb01"], [("c4", "c", 1, 0, 0, 32), ("c5", "c", 1, 0, top, rest)]]
        table["p2"] = [["p2"], [("zb20", "z", 0, 2, 0, 32), ("c6", "c", 0, 2, 0, 64)]]
        table["m2"] = [["m2"], [("zb21", "z", 0, 2, top, rest), ("c7", "c", 0, 2, 64, 64)]]
        table["p3"] = [["p3"], [("p4", "p", 1, 3, 32, 32), ("c8", "c", 1, 3, lo, n)]]
        table["m3"] = [["m3"], [("m4", "m", 1, 1, 64, top - 64), ("c9", "c", 1, 1, lo, n)]]
        table["zb3"] = [["zb30", "zb31"], [("c10", "c", 1, 3, 0, 32), ("c11", "c", 1, 3, top, rest)]]
        table["zb1"] = [["zb10", "zb11"], [("c12", "c", 1, 1, 0, 32), ("c13", "c", 1, 1, top, rest)]]
        table["p4"] = [["p4"], [("c14", "c", 1, 2, 32, 32)]]
        table["m4"] = [["m4"], [("c15", "c", 1, 2, 64, top - 64)]]
        table["zb2"] = [["zb20", "zb21"], [("c16", "c", 1, 2, 0, 32), ("c17", "c", 1, 2, top, rest)]]
        table["in10"] = [["c3", "c4", "c5"], []]
        table["in13"] = [["c8", "c10", "c11"], []]
        table["in11"] = [["c9", "c12", "c13"], []]
        table["in12"] = [["c14", "c15", "c16", "c17"], []]

    def action(waits, sends):
        def act():
            net.got(*[tag + name for name in waits])
            for copy in sends:
                send(*copy)

        return act

    return {tag + name: action(*row) for name, row in table.items()}


N_SCATTER = 29
INBOX_ROWS = 896
PAIRS = [(1, 2), (1, 1), (1, 3), (1, 0), (0, 2), (0, 1), (0, 3), (0, 0)]


def scatter_scratch(w):
    return [
        pltpu.VMEM((16, 128, w), BF),
        pltpu.VMEM((8, 128, w), BF),
        pltpu.VMEM((INBOX_ROWS, w), BF),
    ]


class Scatter:
    def __init__(self, net, pos, part, sib, inbox, tag, top):
        self.net, self.pos, self.part, self.sib, self.tag = net, pos, part, sib, tag
        self.top = top
        self.box, at = {}, 0
        if top == 0:
            rows = [(side + step, n) for step, n in zip("4321", (64, 128, 64, 128)) for side in "pm"]
            rows.append(("z0", 128))
        else:
            rows = [("zb%d%d" % (dy, h), (32, 128 - top)[h]) for dy in range(4) for h in range(2)]
            rows += [("p4", top - 64), ("m4", 32)]
            rows += [(side + step, n) for step, n in zip("321", (top - 32, 64, 128)) for side in "pm"]
            rows.append(("z0", top - 32))
        for key, n in rows:
            self.box[key] = inbox.at[pl.ds(at, n)]
            at += n
        for side in "pm":
            whole = self.box[side + "1"]
            if top:
                self.box[side + "1a"] = whole.at[pl.ds(32, top - 32)]
                self.box[side + "1b"] = whole.at[pl.ds(0, 32)]
                self.box[side + "1c"] = whole.at[pl.ds(top, 128 - top)]

    def mine(self, dz, dy, lo=0, n=128):
        return self.part.at[slot_at(self.pos, dz, dy), pl.ds(lo, n)]

    def swap(self, dz, dy):
        src = self.part.at[slot_at(self.pos, dz, dy, 1)]
        self.net.start(self.tag + "c%d%d" % (dz, dy), "c", src, self.sib.at[dz * 4 + dy])

    def joined(self, dz, dy):
        self.got("c%d%d" % (dz, dy))
        add_to(self.mine(dz, dy), self.sib.at[dz * 4 + dy])

    def got(self, *names):
        self.net.got(*[self.tag + name for name in names])

    def put(self, name, link, *rows):
        self.net.start(self.tag + name, link, self.mine(*rows), self.box[name])

    def put_zb(self, dy):
        self.put("zb%d0" % dy, "z", 1, dy, 0, 32)
        self.put("zb%d1" % dy, "z", 1, dy, self.top, 128 - self.top)

    def take(self, name, dz, dy, lo, n):
        self.got(name)
        add_to(self.mine(dz, dy, lo, n), self.box[name])

    def take_zb(self, dy):
        self.take("zb%d0" % dy, 0, dy, 0, 32)
        self.take("zb%d1" % dy, 0, dy, self.top, 128 - self.top)

    def actions(self):
        act = {
            "j%d%d" % pair: functools.partial(self.joined, *pair)
            for pair in PAIRS
        }

        def does(*steps):
            def run():
                for step, *args in steps:
                    step(*args)

            return run

        put, take, top = self.put, self.take, self.top
        if top == 0:
            act["s4"] = does((put, "p4", "p", 1, 2, 64, 64), (put, "m4", "m", 1, 2, 0, 64))
            act["s2"] = does((put, "p2", "p", 0, 2, 64, 64), (put, "m2", "m", 0, 2, 0, 64))
            act["tp4"] = does((take, "p4", 1, 1, 64, 64), (put, "p3", "p", 1, 1))
            act["tm4"] = does((take, "m4", 1, 3, 0, 64), (put, "m3", "m", 1, 3))
            act["tp2"] = does((take, "p2", 0, 1, 64, 64), (put, "p1", "p", 0, 1))
            act["tm2"] = does((take, "m2", 0, 3, 0, 64), (put, "m1", "m", 0, 3))
            act["tp3"] = does((take, "p3", 1, 0, 0, 128))
            act["tm3"] = does((take, "m3", 1, 0, 0, 128))
            act["sz0"] = does((put, "z0", "z", 1, 0))
            act["tz0"] = does((take, "z0", 0, 0, 0, 128))
            act["last"] = does((self.got, "p1", "m1"))
        else:
            n, rest = top - 32, 128 - top
            for dy in range(4):
                act["szb%d" % dy] = does((self.put_zb, dy))
            act["s4"] = does(
                (put, "p4", "p", 1, 2, 64, top - 64), (put, "m4", "m", 1, 2, 32, 32)
            )
            act["tp4"] = does((take, "p4", 1, 1, 64, top - 64), (put, "p3", "p", 1, 1, 32, n))
            act["tm4"] = does((take, "m4", 1, 3, 32, 32), (put, "m3", "m", 1, 3, 32, n))
            act["tzb2"] = does(
                (self.take_zb, 2), (put, "p2", "p", 0, 2, 64, 64), (put, "m2", "m", 0, 2, 0, 64)
            )
            act["tp3"] = does((take, "p3", 1, 0, 32, n))
            act["tm3"] = does((take, "m3", 1, 0, 32, n))
            act["sz0"] = does((put, "z0", "z", 1, 0, 32, n))
            act["tp2"] = does((take, "p2", 0, 1, 64, 64), (put, "p1a", "p", 0, 1, 32, n))
            act["tm2"] = does((take, "m2", 0, 3, 0, 64), (put, "m1a", "m", 0, 3, 32, n))
            act["tzb1"] = does(
                (self.take_zb, 1), (put, "p1b", "p", 0, 1, 0, 32), (put, "p1c", "p", 0, 1, top, rest)
            )
            act["tzb3"] = does(
                (self.take_zb, 3), (put, "m1b", "m", 0, 3, 0, 32), (put, "m1c", "m", 0, 3, top, rest)
            )
            act["tz0"] = does((take, "z0", 0, 0, 32, n))
            act["tzb0"] = does((self.take_zb, 0))
            act["last"] = does((self.got, "p1a", "m1a", "p1b", "p1c", "m1b", "m1c"))
        return {self.tag + name: run for name, run in act.items()}

    def total(self, cols):
        sums = self.mine(0, 0)[:, cols].astype(F32)
        return sums + self.box["p1"][:, cols].astype(F32) + self.box["m1"][:, cols].astype(F32)


def pair_rows(pos, dz, dy):
    first = slot_at(pos, dz, dy) // 2
    return first * 2, pl.ds(pl.multiple_of(first * 256, 256), 256)


def product(pos, part, dz, dy, *factors):
    slot, rows = pair_rows(pos, dz, dy)

    def tile(cols):
        total = None
        for a, b in factors:
            term = dot(a[rows, :], b[:, cols])
            total = term if total is None else total + term
        part[slot, :, cols] = total[:128].astype(BF)
        part[slot + 1, :, cols] = total[128:].astype(BF)

    apart(lambda: columns(part.shape[2], tile))


def quarter(pos, d, half=None):
    start = ((pos[4] + d) % 4) * 256
    if half is None:
        return pl.ds(pl.multiple_of(start, 256), 256)
    return pl.ds(pl.multiple_of(start + half * 128, 128), 128)


def part_columns(pos, d, p):
    return pl.ds(pl.multiple_of(((pos[4] + d) % 4) * 512 + p * 256, 256), 256)


def by_rows(rows, body):
    step = 352 if rows % 352 == 0 else 128
    for at in range(0, rows, step):
        body(slice(at, at + step))


def ring_sum_scratch(rows):
    return [pltpu.VMEM((2, rows, 128), BF), pltpu.VMEM((2, rows, 256), BF)]


N_RING_SUM = 4
N_RING_SHARE = 5


class Ring:
    def __init__(self, net, pos, tag):
        self.net, self.pos, self.tag = net, pos, tag

    def put(self, name, link, src, dst):
        self.net.start(self.tag + name, link, src, dst)

    def got(self, *names):
        self.net.got(*[self.tag + name for name in names])

    def far(self, terms, far):
        self.put("e2", "e", terms.at[:, quarter(self.pos, 2, 0)], far.at[0])
        self.put("w2", "w", terms.at[:, quarter(self.pos, 2, 1)], far.at[1])

    def near(self, terms, far, near, half):
        name, d = (("e", 1), ("w", 3))[half]
        self.got(name + "2")
        cols = quarter(self.pos, d, half)

        def fold(r):
            terms[r, cols] = terms[r, cols] + far[half, r, :]

        apart(lambda: by_rows(terms.shape[0], fold))
        self.put(name + "1", name, terms.at[:, quarter(self.pos, d)], near.at[half])

    def join(self, terms, near, chunk):
        self.got("e1", "w1")

        def add(r):
            total = terms[r, quarter(self.pos, 0)].astype(F32) + near[0, r, :].astype(F32)
            chunk[r, :] = (total + near[1, r, :].astype(F32)).astype(BF)

        apart(lambda: by_rows(terms.shape[0], add))

    def across(self, chunk, box):
        self.put("h", "h", chunk, box)

    def crossed(self, chunk, box, whole):
        self.got("h")
        cols = quarter(self.pos, 0)

        def add(r):
            whole[r, cols] = chunk[r, :] + box[r, :]

        apart(lambda: by_rows(whole.shape[0], add))
        for name in "ew":
            self.put(name + "3", name, whole.at[:, cols], whole.at[:, cols])

    def share(self, whole, half):
        name, d = (("e", 3), ("w", 1))[half]
        self.got(name + "3")
        ref = whole.at[:, quarter(self.pos, d, half)]
        self.put(name + "4", name, ref, ref)

    def shared(self):
        self.got("e4", "w4")

    def sum_actions(self, terms, far, near, chunk):
        t = self.tag
        return {
            t + "far": functools.partial(self.far, terms, far),
            t + "ne": functools.partial(self.near, terms, far, near, 0),
            t + "nw": functools.partial(self.near, terms, far, near, 1),
            t + "join": functools.partial(self.join, terms, near, chunk),
        }

    def share_actions(self, chunk, box, whole):
        t = self.tag
        return {
            t + "across": functools.partial(self.across, chunk, box),
            t + "crossed": functools.partial(self.crossed, chunk, box, whole),
            t + "se": functools.partial(self.share, whole, 0),
            t + "sw": functools.partial(self.share, whole, 1),
            t + "shared": self.shared,
        }


def sems(n):
    return [pltpu.SemaphoreType.DMA((n,)), pltpu.SemaphoreType.DMA((n,))]


HBM = pl.BlockSpec(memory_space=pl.ANY)


class Moves:
    def __init__(self, fetched, stored, in_sem, out_sem):
        self.fetched, self.stored, self.in_sem, self.out_sem = fetched, stored, in_sem, out_sem
        self.coming, self.going = {}, []
        for n, (name, (far, here)) in enumerate(fetched.items()):
            self.coming[name] = pltpu.make_async_copy(far, here, in_sem.at[n])
            self.coming[name].start()

    def need(self, *names):
        for name in names:
            if name in self.coming:
                self.coming.pop(name).wait()

    def store(self, *names, at=None):
        for name in names:
            here, far = self.stored[name]
            if at is not None:
                here, far = here.at[at], far.at[at]
            copy = pltpu.make_async_copy(here, far, self.out_sem.at[len(self.going)])
            copy.start()
            self.going.append(copy)

    def finish(self):
        for copy in self.going:
            copy.wait()


def call(kernel, name, cid, outs, scratch, args, mib=60, fetched=(), stored=(), n_store=0, in_place=()):
    n_in, n_out = len(args), len(outs)

    def body(*refs):
        ins, results = list(refs[:n_in]), list(refs[n_in : n_in + n_out])
        rest = list(refs[n_in + n_out :])
        out_sem, in_sem = rest.pop(), rest.pop()
        coming, going = {}, {}
        for i in reversed(stored):
            far, results[i] = results[i], rest.pop()
            going[i] = results[i], far
        for i in reversed(fetched):
            far, ins[i] = ins[i], rest.pop()
            coming[i] = far, ins[i]
        moves = Moves(coming, going, in_sem, out_sem)
        kernel(*ins, *results, *rest, moves)
        moves.finish()

    shapes = [jax.ShapeDtypeStruct(s, d) for s, d in outs]
    return pl.pallas_call(
        body,
        out_shape=shapes,
        in_specs=[HBM if i in (*fetched, *in_place) else VM for i in range(n_in)],
        out_specs=[HBM if i in stored else VM for i in range(n_out)],
        scratch_shapes=list(scratch)
        + [pltpu.VMEM(args[i].shape, args[i].dtype) for i in fetched]
        + [pltpu.VMEM(*outs[i]) for i in stored]
        + [pltpu.SemaphoreType.DMA((max(1, len(fetched)),))]
        + [pltpu.SemaphoreType.DMA((max(1, n_store),))],
        compiler_params=pltpu.CompilerParams(
            collective_id=cid, has_side_effects=True, vmem_limit_bytes=mib * 2**20
        ),
        name=name,
    )(*args)


def norm_factor(u):
    return lax.rsqrt(jnp.mean(u * u, -1, keepdims=True) + EPSILON)


def norm_back(u, gain, e):
    f = norm_factor(u)
    scaled = e * gain
    return f * scaled - u * f * f * f * jnp.mean(scaled * u, -1, keepdims=True), u * f


def scattered(sums, me, rows):
    total = sums.part[me, rows, :].astype(F32)
    return total + sums.box["p1"][rows, :].astype(F32) + sums.box["m1"][rows, :].astype(F32)


def by_rows_of_block(body):
    for at in range(0, 128, 32):
        body(slice(at, at + 32))


def rope(u, cosine, sine):
    return u * cosine + pltpu.roll(u, 64, 1) * sine


def block_start(c, half):
    return c * 64 if half == 0 else (31 - c) * 64


def document_start(position, lens):
    first = lens[0:1, 0:1]
    return jnp.where(position >= first, first, 0)


def bias_at(position, lens):
    own = jnp.where(position >= lens[0:1, 0:1], lens[0:1, 1:2], lens[0:1, 0:1])
    return -jnp.log(own.astype(F32))


PROJECT_ORDER = [
    12, 10, 26, 21, 9, 8, 32, 27, 31, 22, 16, 11, 17, 14, 1, 13, 0, 23, 28, 3, 4, 33, 29, 35, 24, 15, 2,
    20, 7, 25, 30, 18, 34, 5, 19, 6,
]


def project_kernel(
    x,
    gain_attn,
    gain_mlp,
    lens,
    w_query,
    w_key,
    w_value,
    w_gate_t,
    w_up_t,
    w_down,
    normed,
    qkv,
    cosines,
    sines,
    gain_rows,
    w_t,
    ff_in,
    ff_out,
    buf,
    gain_box,
    w,
    send,
    recv,
    moves,
):
    pos = place()
    net = Copies(pos, send, recv)
    me = lax.axis_index(CTX)
    buf[me] = x[...]
    gain_box[me] = jnp.zeros((8, 128), F32)
    gain_box[me, 0:1, :] = gain_attn[...].astype(F32)
    gain_box[me, 1:2, :] = gain_mlp[...].astype(F32)
    greet([ctx_peer(d) for d in range(1, 16)])
    for d in range(1, 16):
        ref = gain_box.at[me]
        net.start("g%d" % d, ctx_peer(d), ref, ref)

    def tables():
        lane = lax.broadcasted_iota(jnp.int32, (8, 128), 1) % 64
        frequency = jnp.ones((8, 128), F32)
        for bit in range(6):
            factor = 10000.0 ** (-(2.0**bit) / 64)
            frequency = frequency * jnp.where(lane // 2**bit % 2 == 1, factor, 1.0)

        def table(i, _):
            r = pl.ds(pl.multiple_of(i * 256, 256), 256)
            position = lax.broadcasted_iota(jnp.int32, (256, 128), 0) + i * 256
            offset = position - document_start(position, lens)
            angle = offset.astype(F32) * frequency[0:1, :]
            lane = lax.broadcasted_iota(jnp.int32, (256, 128), 1)
            cosines[r, :] = jnp.cos(angle)
            sines[r, :] = jnp.where(lane < 64, -1.0, 1.0) * jnp.sin(angle)
            return 0

        lax.fori_loop(0, 8, table, 0)
        moves.store(2, 3)

    def weights():
        for i, ref in enumerate((w_query, w_key, w_value)):
            w[:, i * 128 : (i + 1) * 128] = ref[...]
        w_t[...] = w[...].T
        moves.store(5)

    def pads():
        for i, ref in enumerate((w_gate_t, w_up_t)):
            pad_rows(ff_in.at[i], ref)
        pad_rows(ff_out, w_down)
        moves.store(6, 7)

    def gains_in():
        net.got(*["g%d" % d for d in range(1, 16)])
        for j in range(16):
            gain_rows[:, j * 128 : (j + 1) * 128] = gain_box[j]

    def pair(dz, dy):
        slot, _ = pair_rows(pos, dz, dy)

        @apart
        def _():
            for i in range(8):
                r = slice(i % 4 * 32, i % 4 * 32 + 32)
                u = buf[slot + i // 4, r, :].astype(F32)
                n = u * norm_factor(u) * gain_rows[0:1, :]
                normed[slot + i // 4, r, :] = n.astype(BF)

        moves.store(0, at=pl.ds(slot, 2))

        @apart
        def _():
            out = dot(normed[pl.ds(slot, 2)].reshape(256, 2048), w[...])
            for b in range(2):
                for half in range(2):
                    at = pl.ds(pl.multiple_of(block_start(slot + b, half), 64), 64)
                    rows = slice(b * 128 + half * 64, b * 128 + half * 64 + 64)
                    c, s = cosines[at, :], sines[at, :]
                    qkv[0, at, :] = rope(out[rows, :128], c, s).astype(BF)
                    qkv[1, at, :] = rope(out[rows, 128:256], c, s).astype(BF)
                    qkv[2, at, :] = out[rows, 256:].astype(BF)

    actions = gather_actions(net, pos, buf, "x", 96)
    actions.update(tables=tables, weights=weights, pads=pads, gains=gains_in)
    for p in PAIRS:
        actions["a%d%d" % p] = functools.partial(pair, *p)
    perform(actions, PROJECT_ORDER)
    moves.store(1)
    net.finish()


def pad_rows(dst, src):
    rows = src.shape[0]
    dst[pl.ds(0, rows), :] = src[...]
    dst[pl.ds(rows, FF_PAD - rows), :] = jnp.zeros((FF_PAD - rows, dst.shape[1]), BF)


def project(*args):
    return call(
        project_kernel,
        "project",
        0,
        [
            ((16, 128, 2048), BF),
            ((3, 2048, 128), BF),
            ((2048, 128), F32),
            ((2048, 128), F32),
            ((8, 2048), F32),
            ((384, 2048), BF),
            ((2, FF_PAD, 2048), BF),
            ((FF_PAD, 2048), BF),
        ],
        [
            pltpu.VMEM((16, 128, 2048), BF),
            pltpu.VMEM((16, 8, 128), F32),
            pltpu.VMEM((2048, 384), BF),
        ]
        + sems(N_GATHER + 15),
        args,
        stored=(0, 1, 2, 3, 5, 6, 7),
        n_store=14,
    )


SCALE = 1.0 / math.sqrt(128)


def attend_block(qkv, lens, i):
    q = qkv[0, 256 * i : 256 * (i + 1), :]
    row = lax.broadcasted_iota(jnp.int32, (256, 1), 0) + 256 * i
    start = document_start(row, lens)
    bias = bias_at(row, lens)
    total = jnp.zeros((256, 128), F32)
    for lo in range(0, 256 * (i + 1), 512):
        n = min(512, 256 * (i + 1) - lo)
        score = dot_t(q, qkv[1, lo : lo + n, :]) * SCALE + bias
        col = lax.broadcasted_iota(jnp.int32, (1, n), 1) + lo
        visible = col >= start
        if lo + n > 256 * i:
            visible = visible & (col <= row)
        prob = jnp.where(visible, jax.nn.sigmoid(score), 0.0).astype(BF)
        total = total + dot(prob, qkv[2, lo : lo + n, :])
    return total


def packed_start(block):
    return block * 128 if block < 16 else (31 - block) * 128 + 64


MIDDLE_TOPS = (96, 96, 96, 96)
MIDDLE_ORDER = [
    34, 98, 99, 100, 101, 102, 103, 104, 48, 43, 105, 5, 6, 14, 3, 21, 1, 7, 53, 0, 17, 4, 2, 9, 10, 15,
    12, 49, 32, 19, 13, 25, 28, 22, 8, 26, 20, 11, 27, 23, 45, 24, 33, 31, 18, 50, 46, 30, 51, 29, 16,
    67, 114, 128, 44, 123, 52, 134, 133, 35, 54, 57, 130, 56, 55, 125, 39, 47, 124, 119, 63, 36, 126,
    131, 129, 76, 37, 117, 116, 61, 136, 127, 132, 60, 121, 38, 41, 115, 65, 137, 135, 59, 42, 40, 78,
    118, 120, 85, 81, 64, 83, 62, 74, 77, 84, 73, 96, 92, 122, 66, 110, 68, 79, 89, 111, 90, 86, 75,
    108, 112, 87, 70, 71, 113, 91, 95, 88, 106, 97, 82, 72, 107, 109, 93, 94, 80, 58, 69,
]


def middle_kernel(
    qkv,
    lens,
    w_out,
    cot,
    acts,
    gains,
    ff_in,
    ff_out,
    attended,
    residual,
    d_res,
    gain_part,
    hidden,
    chunk,
    later,
    cot_all,
    buf,
    low_t,
    part,
    sib,
    inbox,
    terms,
    far,
    near,
    send,
    recv,
    moves,
):
    pos = place()
    net = Copies(pos, send, recv)
    me = lax.axis_index(CTX)
    cot_all[me] = cot[...]
    greet([neighbour(pos, l) for l in "pmzcew"])
    branch = Scatter(net, pos, part, sib, inbox, "a", MIDDLE_TOPS[1])
    sums = Scatter(net, pos, part, sib, inbox, "s", MIDDLE_TOPS[3])

    def attend(i):
        apart(lambda: attend_rows(i))

    def attend_rows(i):
        out = attend_block(qkv, lens, i).astype(BF)
        for b in range(4):
            at = packed_start(4 * i + b)
            attended[at : at + 64, :] = out[64 * b : 64 * (b + 1)]

    def project_out(dz, dy):
        product(pos, part, dz, dy, (attended, w_out))
        branch.swap(dz, dy)

    def normalise():
        def rows(r):
            u = acts[r, :].astype(F32) + scattered(branch, me, r)
            residual[r, :] = u
            buf[me, r, :] = (u * norm_factor(u) * gains[1:2, :]).astype(BF)

        apart(lambda: by_rows_of_block(rows))
        net.finish()
        moves.store(0, 1)
        moves.need(6, 7)

    def feed_forward(dz, dy):
        slot, rows = pair_rows(pos, dz, dy)

        @apart
        def _():
            n2 = buf[pl.ds(slot, 2)].reshape(256, 2048)
            ct = cot_all[pl.ds(slot, 2)].reshape(256, 2048)
            gate = dot_t(n2, ff_in[0])
            up = dot_t(n2, ff_in[1])
            d_hidden = dot_t(ct, ff_out[...])
            sig = jax.nn.sigmoid(gate)
            silu = gate * sig
            h = (silu * up).astype(BF)
            dg = (d_hidden * up * sig * (1.0 + gate * (1.0 - sig))).astype(BF)
            du = (d_hidden * silu).astype(BF)
            hidden[rows, :] = h
            low_t[0, :, rows] = dg.T
            low_t[1, :, rows] = du.T
            low_t[2, :, rows] = h.T

            def tile(cols):
                t = dot(dg, ff_in[0, :, cols]) + dot(du, ff_in[1, :, cols])
                part[slot, :, cols] = t[:128].astype(BF)
                part[slot + 1, :, cols] = t[128:].astype(BF)

            columns(2048, tile)

        sums.swap(dz, dy)

    def weight_grads(d, p):
        cols, to = part_columns(pos, d, p), quarter(pos, d)
        dst = (terms, later)[p]

        @apart
        def _():
            for i, other in ((0, buf), (1, buf), (2, cot_all)):
                g = dot(low_t[i], other[:, :, cols].reshape(2048, 256))
                dst[pl.ds(i * FF_ROWS, FF_ROWS), to] = g[:FF_ROWS].astype(BF)

    def finish():
        moves.store(4, 6)
        gain_part[...] = jnp.zeros_like(gain_part)

        def rows(r):
            e = scattered(sums, me, r)
            grad, unit = norm_back(residual[r, :], gains[1:2, :], e)
            d_res[r, :] = cot[r, :].astype(F32) + grad
            gain_part[...] += jnp.sum(e * unit, 0, keepdims=True)

        apart(lambda: by_rows_of_block(rows))

    actions = gather_actions(net, pos, cot_all, "c", MIDDLE_TOPS[0])
    actions.update(gather_actions(net, pos, buf, "x", MIDDLE_TOPS[2]))
    actions.update(branch.actions())
    actions.update(sums.actions())
    actions.update(Ring(net, pos, "r").sum_actions(terms, far, near, chunk))
    for i in range(8):
        actions["t%d" % i] = functools.partial(attend, i)
    for p in PAIRS:
        actions["aP%d%d" % p] = functools.partial(project_out, *p)
        actions["m%d%d" % p] = functools.partial(feed_forward, *p)
    for d in range(4):
        for p in range(2):
            actions["w%d%d" % (d, p)] = functools.partial(weight_grads, d, p)
    actions.update(norm=normalise, fin=finish)
    perform(actions, MIDDLE_ORDER)
    moves.store(5)
    net.finish()


def middle(*args):
    return call(
        middle_kernel,
        "middle",
        1,
        [
            ((2048, 128), BF),
            ((128, 2048), F32),
            ((128, 2048), F32),
            ((1, 2048), F32),
            ((2048, FF_PAD), BF),
            ((3 * FF_ROWS, 256), BF),
            ((3 * FF_ROWS, 1024), BF),
        ],
        [pltpu.VMEM((16, 128, 2048), BF), pltpu.VMEM((16, 128, 2048), BF)]
        + [pltpu.VMEM((3, FF_PAD, 2048), BF)]
        + scatter_scratch(2048)
        + [pltpu.VMEM((3 * FF_ROWS, 1024), BF)]
        + ring_sum_scratch(3 * FF_ROWS)
        + sems(2 * N_SCATTER + 2 * N_GATHER + N_RING_SUM),
        args,
        62,
        fetched=(6, 7),
        stored=(0, 1, 4, 5, 6),
        n_store=5,
    )


BACK_TOPS = (112, 0, 0)
BACK_ORDER = [
    118, 47, 103, 45, 56, 48, 132, 46, 57, 43, 105, 137, 127, 133, 55, 60, 138, 122, 42, 119, 96, 128,
    106, 130, 41, 134, 129, 120, 141, 123, 18, 135, 67, 97, 126, 25, 44, 64, 51, 139, 104, 52, 22, 121,
    136, 131, 140, 124, 101, 23, 125, 59, 19, 24, 54, 20, 98, 21, 100, 32, 66, 33, 53, 63, 61, 34, 35,
    102, 50, 65, 62, 36, 37, 38, 39, 27, 40, 113, 114, 116, 112, 111, 68, 115, 110, 2, 58, 49, 117, 26,
    75, 11, 72, 5, 71, 83, 87, 4, 69, 74, 76, 79, 86, 14, 13, 82, 29, 99, 70, 3, 107, 84, 91, 80, 78,
    109, 94, 0, 73, 12, 81, 9, 92, 1, 30, 10, 93, 89, 90, 88, 31, 6, 8, 108, 15, 77, 17, 95, 7, 85, 16,
    28,
]


def back_kernel(
    d_res,
    attended,
    w_out,
    chunk0,
    later,
    qkv,
    lens,
    cosines,
    sines,
    hidden,
    ff_out,
    residual,
    w_t,
    far_normed,
    acts,
    gains_in,
    gain_two_part,
    mixed,
    ff_sums,
    acts_grad,
    attn_sums,
    gains,
    buf,
    part,
    sib,
    inbox,
    ff_far,
    ff_near,
    chunk1,
    ff_box,
    total,
    do,
    dq,
    d_qkv,
    low_t,
    terms,
    chunk,
    box,
    far0,
    near0,
    far1,
    near1,
    gain_terms,
    gain_box,
    gain_sum,
    gain_wide,
    send,
    recv,
    in_sem,
    free_sem,
    moves,
):
    pos = place()
    net = Copies(pos, send, recv)
    me = lax.axis_index(CTX)
    buf[me] = d_res[...].astype(BF)
    total[...] = jnp.zeros_like(total)
    dq[...] = jnp.zeros_like(dq)
    gain_terms[...] = jnp.zeros_like(gain_terms)
    for j in range(16):
        gain_terms[j, 0:1, :] = gain_two_part[:, j * 128 : (j + 1) * 128]
    greet([ctx_peer(d) for d in range(1, 16)] + [grp_peer(d) for d in range(1, 8)])
    outs = Scatter(net, pos, part, sib, inbox, "s", BACK_TOPS[1])
    sums = Scatter(net, pos, part, sib, inbox, "t", BACK_TOPS[2])
    fetch = pltpu.make_async_copy(far_normed, buf, in_sem)

    def branch_rows(dz, dy):
        slot, rows = pair_rows(pos, dz, dy)
        moves.need(1)

        @apart
        def _():
            d = buf[pl.ds(slot, 2)].reshape(256, 2048)
            g = dot_t(d, w_out[...]).astype(BF)
            for b in range(2):
                for half in range(2):
                    at = pl.ds(pl.multiple_of(block_start(slot + b, half), 64), 64)
                    do[at, :] = g[b * 128 + half * 64 : b * 128 + half * 64 + 64]
            total[...] += t_dot(attended[rows, :], d)

    def feed_out(dz, dy):
        moves.need(9, 10)
        product(pos, part, dz, dy, (hidden, ff_out))
        outs.swap(dz, dy)

    def put(block, value, i):
        for b in range(4):
            at = packed_start(4 * block + b)
            d_qkv[at : at + 64, 128 * i : 128 * (i + 1)] = value[64 * b : 64 * (b + 1)]

    def unrotate(u, block):
        r = slice(256 * block, 256 * (block + 1))
        return rope(u * SCALE, cosines[r, :], -sines[r, :]).astype(BF)

    def keys(j):
        mine = slice(256 * j, 256 * (j + 1))
        k, v = qkv[1, mine, :], qkv[2, mine, :]
        row = lax.broadcasted_iota(jnp.int32, (256, 1), 0) + 256 * j
        dk = jnp.zeros((256, 128), F32)
        dv = jnp.zeros((256, 128), F32)
        for lo in range(256 * j, 2048, 512):
            n = min(512, 2048 - lo)
            rows = slice(lo, lo + n)
            col = lax.broadcasted_iota(jnp.int32, (1, n), 1) + lo
            q, d = qkv[0, rows, :], do[rows, :]
            sig = jax.nn.sigmoid(dot_t(k, q) * SCALE + bias_at(col, lens))
            visible = row >= document_start(col, lens)
            if lo == 256 * j:
                visible = visible & (row <= col)
            sig = jnp.where(visible, sig, 0.0)
            dv = dv + dot(sig.astype(BF), d)
            ds = (dot_t(v, d) * sig * (1.0 - sig)).astype(BF)
            dk = dk + dot(ds, q)
            dq[rows, :] += t_dot(ds, k)
        put(j, unrotate(dk, j), 1)
        put(j, dv.astype(BF), 2)

    def key_rows(j):
        if j == 0:
            moves.need(5, 7, 8)
        apart(functools.partial(keys, j))

    def queries():
        moves.need(12)

        @apart
        def _():
            for i in range(8):
                put(i, unrotate(dq[256 * i : 256 * (i + 1), :], i), 0)

        @apart
        def _():
            low_t[...] = d_qkv[...].T
            for p in range(2):
                for q in range(4):
                    cols = slice(q * 512 + p * 256, q * 512 + p * 256 + 256)
                    terms[p, 384:512, q * 256 : (q + 1) * 256] = total[:, cols].astype(BF)

        for name in [n for n in net.unsent if n.startswith("x")]:
            net.sent(name)
        fetch.start()

    def outs_done():
        moves.need(11)

        def last(cols):
            mixed[:, cols] = (residual[:, cols] + outs.total(cols)).astype(BF)

        apart(lambda: columns(2048, last))
        moves.store(0)
        for name in [n for n in net.unsent if n.startswith("s")]:
            net.sent(name)
        for link in "pmzc":
            pl.semaphore_signal(
                free_sem, inc=1, device_id=neighbour(pos, link), device_id_type=MESH
            )

    def credit():
        pl.semaphore_wait(free_sem, 4)

    def back_in(dz, dy):
        product(pos, part, dz, dy, (d_qkv, w_t))
        sums.swap(dz, dy)

    def weight_grads(d, p):
        cols = part_columns(pos, d, p)
        first = ((pos[4] + d) % 4) * 4 + p * 2

        @apart
        def _():
            g = dot(low_t[...], buf[:, :, cols].reshape(2048, 256))
            terms[p, 0:384, quarter(pos, d)] = g.astype(BF)
            by_column = jnp.sum(g * w_t[:, cols].astype(F32), 0, keepdims=True)
            by_column = by_column / gains_in[0:1, cols]
            gain_terms[first, 1:2, :] = by_column[:, :128]
            gain_terms[first + 1, 1:2, :] = by_column[:, 128:]

    def after(operand, act):
        moves.need(operand)
        act()

    def ff_done(shared, p):
        shared()
        moves.store(1, at=p)

    def gain_out():
        for d in range(1, 16):
            net.start("g%d" % d, ctx_peer(d), gain_terms.at[(me + d) % 16], gain_box.at[d])
        gain_box[0] = gain_terms[me]

    def gain_across():
        net.got(*["g%d" % d for d in range(1, 16)])
        gain_sum[...] = jnp.sum(gain_box[...], 0)
        for d in range(1, 8):
            net.start("h%d" % d, grp_peer(d), gain_sum, gain_wide.at[d])
        gain_wide[0] = gain_sum[...]

    def gain_in():
        net.got(*["h%d" % d for d in range(1, 8)])
        gains[...] = jnp.sum(gain_wide[...], 0)

    def finish():
        def rows(r):
            grad, _ = norm_back(acts[r, :].astype(F32), gains_in[0:1, :], scattered(sums, me, r))
            acts_grad[r, :] = d_res[r, :] + grad

        apart(lambda: by_rows_of_block(rows))

    actions = gather_actions(net, pos, buf, "x", BACK_TOPS[0])
    actions.update(outs.actions())
    actions.update(sums.actions())
    actions.update(Ring(net, pos, "u").share_actions(chunk0, ff_box.at[0], ff_sums.at[0]))
    ring = Ring(net, pos, "v")
    actions.update(ring.sum_actions(later, ff_far, ff_near, chunk1))
    actions.update(ring.share_actions(chunk1, ff_box.at[1], ff_sums.at[1]))
    for p, far, near in ((0, far0, near0), (1, far1, near1)):
        ring = Ring(net, pos, "UV"[p])
        actions.update(ring.sum_actions(terms.at[p], far, near, chunk.at[p]))
        actions.update(ring.share_actions(chunk.at[p], box.at[p], attn_sums.at[p]))
        for d in range(4):
            actions["w%d%d" % (d, p)] = functools.partial(weight_grads, d, p)
    for p in PAIRS:
        actions["a%d%d" % p] = functools.partial(branch_rows, *p)
        actions["sP%d%d" % p] = functools.partial(feed_out, *p)
        actions["tP%d%d" % p] = functools.partial(back_in, *p)
    for j in range(8):
        actions["k%d" % j] = functools.partial(key_rows, j)
    actions.update(dq=queries, sdone=outs_done, credit=credit, load=fetch.wait)
    actions.update(gain=gain_out, gain2=gain_across, gain3=gain_in, fin=finish)
    for name, operand in (("uacross", 3), ("vfar", 4)):
        actions[name] = functools.partial(after, operand, actions[name])
    for p in range(2):
        shared = actions["uv"[p] + "shared"]
        actions["uv"[p] + "shared"] = functools.partial(ff_done, shared, p)
    perform(actions, BACK_ORDER)
    net.finish()


def back(*args):
    return call(
        back_kernel,
        "back",
        2,
        [
            ((128, 2048), BF),
            ((2, 3 * FF_ROWS, 1024), BF),
            ((128, 2048), F32),
            ((2, 512, 1024), BF),
            ((8, 128), F32),
        ],
        [pltpu.VMEM((16, 128, 2048), BF)]
        + scatter_scratch(2048)
        + ring_sum_scratch(3 * FF_ROWS)
        + [pltpu.VMEM((3 * FF_ROWS, 256), BF), pltpu.VMEM((2, 3 * FF_ROWS, 256), BF)]
        + [
            pltpu.VMEM((128, 2048), F32),
            pltpu.VMEM((2048, 128), BF),
            pltpu.VMEM((2048, 128), F32),
            pltpu.VMEM((2048, 384), BF),
            pltpu.VMEM((384, 2048), BF),
            pltpu.VMEM((2, 512, 1024), BF),
            pltpu.VMEM((2, 512, 256), BF),
            pltpu.VMEM((2, 512, 256), BF),
        ]
        + ring_sum_scratch(512)
        + ring_sum_scratch(512)
        + [
            pltpu.VMEM((16, 8, 128), F32),
            pltpu.VMEM((16, 8, 128), F32),
            pltpu.VMEM((8, 128), F32),
            pltpu.VMEM((8, 8, 128), F32),
        ]
        + sems(N_GATHER + 2 * N_SCATTER + 3 * N_RING_SUM + 4 * N_RING_SHARE + 22)
        + [pltpu.SemaphoreType.DMA, pltpu.SemaphoreType.REGULAR],
        args,
        62,
        fetched=(1, 3, 4, 5, 7, 8, 9, 10, 11, 12),
        stored=(0, 1),
        n_store=3,
        in_place=(13,),
    )


def widen_kernel(
    ff, attn, gains, mixed, acts_grad, gate, up, down, query, key, value, out, one, two, m, g
):
    for i, ref in enumerate((gate, up, down)):
        ref[...] = ff[0, i * FF_ROWS : i * FF_ROWS + ref.shape[0], :].astype(F32)
    for i, ref in enumerate((query, key, value)):
        ref[...] = attn[0, i * 128 : (i + 1) * 128, :].astype(F32).T
    out[...] = attn[0, 384:512, :].astype(F32)
    one[...], two[...] = gains[1:2, :], gains[0:1, :]
    m[...], g[...] = mixed[...], acts_grad[...]


def widen(ff_sums, attn_sums, gains, mixed, acts_grad, ff):
    by_part = lambda j: (j % 2, 0, j // 2)
    column, row, all_of = lambda j: (0, j), lambda j: (j, 0), lambda j: (0, 0)
    block = pl.BlockSpec((128, 256), column)
    return pl.pallas_call(
        widen_kernel,
        grid=(8,),
        out_shape=[jax.ShapeDtypeStruct((ff, 2048), F32)] * 3
        + [jax.ShapeDtypeStruct((2048, 128), F32)] * 3
        + [jax.ShapeDtypeStruct((128, 2048), F32)]
        + [jax.ShapeDtypeStruct((1, 128), F32)] * 2
        + [jax.ShapeDtypeStruct((128, 2048), BF), jax.ShapeDtypeStruct((128, 2048), F32)],
        in_specs=[
            pl.BlockSpec((1, 3 * FF_ROWS, 256), by_part),
            pl.BlockSpec((1, 512, 256), by_part),
            pl.BlockSpec((8, 128), all_of),
            block,
            block,
        ],
        out_specs=[pl.BlockSpec((ff, 256), column)] * 3
        + [pl.BlockSpec((256, 128), row)] * 3
        + [block]
        + [pl.BlockSpec((1, 128), all_of)] * 2
        + [block, block],
        compiler_params=pltpu.CompilerParams(vmem_limit_bytes=62 * 2**20),
        name="widen",
    )(ff_sums, attn_sums, gains, mixed, acts_grad)


def local(
    acts,
    doc_lengths,
    w_query,
    w_key,
    w_value,
    w_out,
    w_gate,
    w_up,
    w_down,
    gain_attn,
    gain_mlp,
    cotangent,
):
    tok = acts.shape[2]
    width = acts.shape[3]
    head = w_query.shape[1]
    ff = w_gate.shape[1]

    acts_rows = acts.reshape(tok, width)
    cot_low = cotangent.reshape(tok, width)
    normed, qkv, cosines, sines, gain_rows, w_t, ff_in, ff_out = project(
        acts_rows,
        gain_attn.reshape(1, head),
        gain_mlp.reshape(1, head),
        doc_lengths,
        w_query,
        w_key,
        w_value,
        w_gate.T,
        w_up.T,
        w_down,
    )
    attended, residual, d_res, gain_two_part, hidden, chunk, later = middle(
        qkv, doc_lengths, w_out, cot_low, acts_rows, gain_rows, ff_in, ff_out
    )
    mixed, ff_sums, acts_grad, attn_sums, gain_grads = back(
        d_res,
        attended,
        w_out,
        chunk,
        later,
        qkv,
        doc_lengths,
        cosines,
        sines,
        hidden,
        ff_out,
        residual,
        w_t,
        normed,
        acts_rows,
        gain_rows,
        gain_two_part,
    )
    gate, up, down, query, key, value, out, one, two, mixed, acts_grad = widen(
        ff_sums, attn_sums, gain_grads, mixed, acts_grad, ff
    )
    return (
        mixed.reshape(1, 1, tok, width),
        acts_grad.reshape(1, 1, tok, width),
        query,
        key,
        value,
        out,
        gate.T,
        up.T,
        down,
        one.reshape(head),
        two.reshape(head),
    )


def solution(mesh):
    row = P(GRP, CTX, None, None)
    col = P(None, CTX)
    dep = P(CTX, None)
    vec = P(CTX)
    in_specs = (row, P(GRP, None), col, col, col, dep, col, col, dep, vec, vec, row)
    out_specs = (row, row, col, col, col, dep, col, col, dep, vec, vec)
    return jax.shard_map(local, mesh=mesh, in_specs=in_specs, out_specs=out_specs, check_vma=False)
```
